32 devices in a mesh: split: 4 (over x, core), tensor: 8 (over z, y).
Axes of the slice: x: 2, y: 2, z: 4, core: 2. Of those that a mesh axis runs over, the one named last changes fastest.
Arguments:
- three_centre: bfloat16 [256, 256, 128], P('split', 'tensor'), may hold values from -6 to 6
- green_occ: bfloat16 [256, 256], P('split'), may hold values from -0.375 to 0.375
- green_virt: bfloat16 [256, 256], P('tensor'), may hold values from -0.375 to 0.375
- occ_mask: int32 [8, 8], replicated, may hold values 0 or 1
- virt_mask: int32 [8, 8], replicated, may hold values 0 or 1
Outputs:
- polar: float32 [128, 128], P('split')
The draws below stay inside these ranges and needn't reach their ends.
All inputs are finite; a program needn't handle non-finite values.
Results may differ from the reference program's by a relative error of at most 0.008.
Values may be sent and summed in bfloat16 or wider, within the bound.
No kernel may reach another device: no remote copies, remote signals or barrier semaphores. Data moves between devices by JAX's collectives and lax.ppermute only.
A program may use at most 128 MiB of HBM per device.

```python
import jax
import jax.numpy as jnp
from jax import lax

BB = 32
AO_DEV = 32
NAUX = 128
NAO = 256
NBK = 8
N_SPLIT = 4
N_TENSOR = 8


def plant(result, rng, smallest, high):
    shape = result.shape
    place = [jax.random.randint(jax.random.fold_in(rng, axis), (), 0, shape[axis]) for axis in range(len(shape))]
    result = result.at[tuple(place)].set(smallest)
    longest = shape.index(max(shape))
    place[longest] = (place[longest] + 1) % shape[longest]
    return result.at[tuple(place)].set(high)


def levels(rng, shape, pieces, low, top_value):
    def one(dim, blocks):
        draws = jax.random.uniform(jax.random.fold_in(jax.random.fold_in(rng, 6), dim), (blocks,), jnp.float32, low / len(pieces), top_value / len(pieces))
        return jnp.repeat(jnp.exp(draws), shape[dim] // blocks).reshape((-1,) + (1,) * (len(shape) - dim - 1))

    level = one(*pieces[0])
    for cut in pieces[1:]:
        level = level * one(*cut)
    return level


def normal_values(key, extent, scale, reach, cuts=(), dtype=jnp.bfloat16):
    result = scale * jax.random.normal(key, extent, jnp.float32)
    if cuts:
        result = result * levels(key, extent, cuts, -0.22, 0.18)
    return jnp.clip(result, -reach, reach).astype(dtype)


def setup_inputs(seed: int = 0) -> dict:
    keys = jax.random.split(jax.random.key(seed), 6)
    three_centre = normal_values(keys[0], (NAO, NAO, NAUX), 1.0, 6.0, ((0, 4), (1, 8)))
    green_occ = normal_values(keys[1], (NAO, NAO), NAO ** -0.5, 0.375, ((0, 4),))
    green_virt = normal_values(keys[2], (NAO, NAO), NAO ** -0.5, 0.375, ((0, 8),))
    occ_mask = plant((jax.random.randint(keys[3], (NBK, NBK), 0, 4) < 3).astype(jnp.int32), jax.random.fold_in(keys[3], 1), 0, 1)
    virt_mask = plant((jax.random.randint(keys[4], (NBK, NBK), 0, 4) < 3).astype(jnp.int32), jax.random.fold_in(keys[4], 1), 0, 1)
    return {"three_centre": three_centre, "green_occ": green_occ, "green_virt": green_virt, "occ_mask": occ_mask, "virt_mask": virt_mask}


def widen(mask, block):
    return jnp.repeat(jnp.repeat(mask, block, axis=0), block, axis=1)


def reference(three_centre, green_occ, green_virt, occ_mask, virt_mask):
    occ = jnp.where(widen(occ_mask, BB) > 0, green_occ, jnp.zeros_like(green_occ))
    virt = jnp.where(widen(virt_mask, BB) > 0, green_virt, jnp.zeros_like(green_virt))
    virt_wide = virt.astype(jnp.float32)
    slice_rows = NAO // N_SPLIT
    total = jnp.zeros((NAUX, NAUX), jnp.float32)
    for index in range(N_SPLIT):
        basis_slice = three_centre[index * slice_rows:(index + 1) * slice_rows].astype(jnp.float32)
        occ_slice = occ[index * slice_rows:(index + 1) * slice_rows].astype(jnp.float32)

        def one_block(start):
            occ_cols = lax.dynamic_slice_in_dim(occ_slice, start, AO_DEV, 1)
            first = jnp.einsum("mn,mlp->nlp", occ_cols, basis_slice).astype(jnp.bfloat16)
            second = jnp.einsum("ls,nlp->nsp", virt_wide, first.astype(jnp.float32)).astype(jnp.bfloat16)
            columns = lax.dynamic_slice_in_dim(three_centre, start, AO_DEV, 1).astype(jnp.float32)
            return jnp.einsum("nsp,snq->pq", second.astype(jnp.float32), columns)

        starts = (jnp.arange(N_TENSOR) * AO_DEV).astype(jnp.int32)
        total = total + jnp.sum(lax.map(one_block, starts), axis=0)
    return total / NAO
```

```python
import functools

import jax
import jax.numpy as jnp
from jax import lax
from jax.experimental import pallas as pl
from jax.experimental.pallas import tpu as pltpu
from jax.sharding import PartitionSpec as P

VMEM_LIMIT = 48 * 1024 * 1024


def swap_blocks(x, width, flag):
    cols = x.shape[1]
    order = []
    for start in range(0, cols, 2 * width):
        order += [x[:, start + width:start + 2 * width], x[:, start:start + width]]
    return jnp.where(flag, jnp.concatenate(order, axis=1), x)


def xor_blocks(x, width, index):
    blocks = x.shape[1] // width
    bit = 1
    while bit < blocks:
        x = swap_blocks(x, width * bit, (index & bit) != 0)
        bit *= 2
    return x


def screened(green, mask_ref, first_row, block):
    rows, cols = green.shape
    column = lax.broadcasted_iota(jnp.int32, (block, cols), 1) // block
    parts = []
    for r in range(rows // block):
        keep = jnp.zeros((block, cols), jnp.int32)
        for c in range(cols // block):
            keep = jnp.where(column == c, mask_ref[first_row + r, c], keep)
        part = green[r * block:(r + 1) * block].astype(jnp.float32)
        parts.append(jnp.where(keep > 0, part, 0.0))
    return jnp.concatenate(parts, axis=0) if len(parts) > 1 else parts[0]


def pack_kernel(n_split, n_tensor, place, occ_mask, virt_mask, b_ref, occ_ref, virt_ref, *outs):
    s, t = place[0], place[1]
    cols, rows, naux = b_ref.shape
    width = naux // n_split
    group = cols // n_split
    block = occ_ref.shape[1] // occ_mask.shape[0]
    occ = screened(occ_ref[...], occ_mask, s * (rows // block), block)
    occ = xor_blocks(occ, cols, t).astype(jnp.bfloat16)
    virt = screened(virt_ref[...], virt_mask, t * (cols // block), block)
    outs[n_split][...] = xor_blocks(virt, rows, s).astype(jnp.bfloat16)
    for m in range(n_split):
        outs[m][:, group * naux:] = occ
    for l in range(group):
        for member in range(n_split):
            lanes = slice(member * width, (member + 1) * width)
            tile = jnp.concatenate([b_ref[j * group + l, :, lanes] for j in range(n_split)], axis=1)
            for m in range(n_split):

                @pl.when((s ^ m) == member)
                def _():
                    outs[m][:, l * naux:(l + 1) * naux] = tile


def first_kernel(n_split, n_tensor, width, *refs):
    packed, outs = refs[:n_split], refs[n_split:]
    whole = jnp.concatenate([p[...] for p in packed], axis=0)
    first = lax.dot_general(
        whole[:, width:], whole[:, :width], (((0,), (0,)), ((), ())), preferred_element_type=jnp.float32
    )
    rows = first.shape[0] // n_tensor
    for k in range(n_tensor):
        outs[k][...] = first[k * rows:(k + 1) * rows].astype(jnp.bfloat16)


def g_kernel(n_split, virt_ref, *refs):
    out = refs[n_split]
    for n in range(out.shape[0]):
        right = jnp.concatenate([r[n] for r in refs[:n_split]], axis=0)
        out[n] = jnp.dot(virt_ref[...], right, preferred_element_type=jnp.float32).astype(jnp.bfloat16)


def last_kernel(n_split, n_tensor, scale, g_ref, *refs):
    firsts, out = refs[:n_tensor], refs[n_tensor]
    rows = firsts[0].shape[0]
    naux = g_ref.shape[2]
    group = firsts[0].shape[1] // naux
    width = naux // n_split
    totals = [jnp.zeros((naux, naux), jnp.float32) for _ in range(n_split)]
    for k in range(n_tensor):
        left = jnp.concatenate([firsts[k][:, l * naux:(l + 1) * naux] for l in range(group)], axis=0)
        for j in range(n_split):
            start = (k * n_split + j) * group
            right = g_ref[start:start + group].reshape(group * rows, naux)
            totals[j] += lax.dot_general(
                left, right, (((0,), (0,)), ((), ())), preferred_element_type=jnp.float32
            )
    result = totals[0][:width]
    for j in range(1, n_split):
        result = result + totals[j][j * width:(j + 1) * width]
    out[...] = result * scale


def local(three_centre, green_occ, green_virt, occ_mask, virt_mask, *, n_split, n_tensor):
    rows, cols, naux = three_centre.shape
    nao = green_occ.shape[1]
    group = cols // n_split
    packed_width = group * naux
    count = n_split * n_tensor
    params = pltpu.CompilerParams(vmem_limit_bytes=VMEM_LIMIT)
    bf16 = jnp.bfloat16

    def exchange(x, split_bits=0, tensor_bits=0):
        bits = split_bits * n_tensor + tensor_bits
        return lax.ppermute(x, ("split", "tensor"), [(d, d ^ bits) for d in range(count)])

    place = jnp.stack([lax.axis_index("split"), lax.axis_index("tensor")]).astype(jnp.int32)
    basis = jnp.swapaxes(three_centre, 0, 1)
    smem = pl.BlockSpec(memory_space=pltpu.SMEM)
    vmem = pl.BlockSpec(memory_space=pltpu.VMEM)
    *packed, virt = pl.pallas_call(
        functools.partial(pack_kernel, n_split, n_tensor),
        out_shape=[jax.ShapeDtypeStruct((rows, packed_width + nao), bf16)] * n_split
        + [jax.ShapeDtypeStruct(green_virt.shape, bf16)],
        in_specs=[smem] * 3 + [vmem] * 3,
        out_specs=[vmem] * (n_split + 1),
        compiler_params=params,
    )(place, occ_mask, virt_mask, basis, green_occ, green_virt)
    packed = [packed[0]] + [exchange(packed[m], split_bits=m) for m in range(1, n_split)]

    held = {0: basis}
    bit = n_split // 2
    while bit:
        held.update({m | bit: exchange(x, split_bits=bit) for m, x in held.items()})
        bit //= 2

    bit = 1
    while bit < n_tensor:
        virt = jnp.concatenate([virt, exchange(virt, tensor_bits=bit)], axis=0)
        bit *= 2

    firsts = pl.pallas_call(
        functools.partial(first_kernel, n_split, n_tensor, packed_width),
        out_shape=[jax.ShapeDtypeStruct((cols, packed_width), bf16)] * n_tensor,
        in_specs=[vmem] * n_split,
        out_specs=[vmem] * n_tensor,
        compiler_params=params,
    )(*packed)
    firsts = [firsts[0]] + [exchange(firsts[k], tensor_bits=k) for k in range(1, n_tensor)]

    step = 8
    g = pl.pallas_call(
        functools.partial(g_kernel, n_split),
        grid=(cols // step,),
        out_shape=jax.ShapeDtypeStruct((cols, nao, naux), bf16),
        in_specs=[pl.BlockSpec((nao, nao), lambda i: (0, 0))]
        + [pl.BlockSpec((step, rows, naux), lambda i: (i, 0, 0))] * n_split,
        out_specs=pl.BlockSpec((step, nao, naux), lambda i: (i, 0, 0)),
        compiler_params=params,
    )(virt, *[held[m] for m in range(n_split)])
    g = jnp.swapaxes(g, 0, 1)

    total = pl.pallas_call(
        functools.partial(last_kernel, n_split, n_tensor, 1.0 / nao),
        out_shape=jax.ShapeDtypeStruct((naux // n_split, naux), jnp.float32),
        in_specs=[vmem] * (1 + n_tensor),
        out_specs=vmem,
        compiler_params=params,
    )(g, *firsts)
    bit = 1
    while bit < n_tensor:
        total = total + exchange(total, tensor_bits=bit)
        bit *= 2
    return total


def solution(mesh):
    sizes = dict(mesh.shape)
    return jax.shard_map(
        functools.partial(local, n_split=sizes["split"], n_tensor=sizes["tensor"]),
        mesh=mesh,
        in_specs=(P("split", "tensor", None), P("split", None), P("tensor", None), P(), P()),
        out_specs=P("split", None),
        check_vma=False,
    )
```

```python
import functools

import jax
import jax.numpy as jnp
from jax import lax
from jax.experimental import pallas as pl
from jax.experimental.pallas import tpu as pltpu
from jax.sharding import PartitionSpec as P

VMEM_LIMIT = 24 * 1024 * 1024
PACK_VMEM_LIMIT = 56 * 1024 * 1024
BF16 = jnp.bfloat16
F32 = jnp.float32


def xor_blocks(x, width, index):
    cols = x.shape[1]
    bit = 1
    while width * bit < cols:
        span = width * bit
        order = []
        for start in range(0, cols, 2 * span):
            order += [x[:, start + span:start + 2 * span], x[:, start:start + span]]
        x = jnp.where((index & bit) != 0, jnp.concatenate(order, axis=1), x)
        bit *= 2
    return x


def screened(green, mask_ref, first_row, block):
    rows, cols = green.shape
    column = lax.broadcasted_iota(jnp.int32, (1, cols), 1) // block
    parts = []
    for r in range(rows // block):
        keep = jnp.zeros((1, cols), jnp.int32)
        for c in range(cols // block):
            keep = jnp.where(column == c, mask_ref[first_row + r, c], keep)
        part = green[r * block:(r + 1) * block].astype(F32)
        parts.append(jnp.where(keep > 0, part, 0.0))
    return jnp.concatenate(parts, axis=0) if len(parts) > 1 else parts[0]


def swap_lane_blocks(tiles, width):
    tiles = list(tiles)
    count = len(tiles)
    lanes = tiles[0].shape[1]
    lane = lax.broadcasted_iota(jnp.int32, tiles[0].shape, 1)
    half = count // 2
    while half:
        span = half * width
        low = (lane // span) % 2 == 0
        for j in range(count):
            if j & half:
                continue
            a, b = tiles[j], tiles[j | half]
            tiles[j] = jnp.where(low, a, pltpu.roll(b, span, 1))
            tiles[j | half] = jnp.where(low, pltpu.roll(a, lanes - span, 1), b)
        half //= 2
    return tiles


def xor_list(items, index):
    bit = 1
    while bit < len(items):
        flag = (index & bit) != 0
        items = [jnp.where(flag, items[m ^ bit], items[m]) for m in range(len(items))]
        bit *= 2
    return items


def pack_kernel(n_split, mask_hbm, b_hbm, occ_hbm, basis_ref, *rest):
    outs, (mask, b, green, sems) = rest[:n_split], rest[n_split:]
    copies = [
        pltpu.make_async_copy(src, dst, sems.at[i])
        for i, (src, dst) in enumerate(((b_hbm, b), (occ_hbm, green), (mask_hbm, mask)))
    ]
    for copy in copies:
        copy.start()
    s, t = lax.axis_index("split"), lax.axis_index("tensor")
    rows, cols, naux = b.shape
    group = cols // n_split
    block = green.shape[1] // mask.shape[0]
    for copy in copies[1:]:
        copy.wait()
    occ = screened(green[...], mask, s * (rows // block), block)
    occ = xor_blocks(occ, cols, t).astype(BF16)
    for m in range(n_split):
        outs[m][:, group * naux:] = occ
    copies[0].wait()
    basis_ref[...] = jnp.swapaxes(b[...], 0, 1)
    for l in range(group):
        tiles = swap_lane_blocks([basis_ref[j * group + l] for j in range(n_split)], naux // n_split)
        tiles = xor_list(tiles, s)
        for m in range(n_split):
            outs[m][:, l * naux:(l + 1) * naux] = tiles[m]


def first_kernel(n_split, n_tensor, width, *refs):
    packed, outs = refs[:n_split], refs[n_split:]
    whole = jnp.concatenate([p[...] for p in packed], axis=0)
    first = lax.dot_general(
        whole[:, width:], whole[:, :width], (((0,), (0,)), ((), ())), preferred_element_type=F32
    )
    rows = first.shape[0] // n_tensor
    for k in range(n_tensor):
        outs[k][...] = first[k * rows:(k + 1) * rows].astype(BF16)


def g_kernel(n_split, n_tensor, mask, virt_ref, *refs):
    out, virt = refs[n_split], refs[n_split + 1]
    part, step = out.shape[0], out.shape[1]
    nao = virt.shape[0]
    cols = nao // n_tensor
    rows = nao // n_split
    block = nao // mask.shape[0]
    s, t = lax.axis_index("split"), lax.axis_index("tensor")

    @pl.when((pl.program_id(0) == 0) & (pl.program_id(1) == 0))
    def _():
        for k in range(n_tensor):
            piece = slice(k * cols, (k + 1) * cols)
            kept = screened(virt_ref[piece, :], mask, (t ^ k) * (cols // block), block)
            virt[piece, :] = xor_blocks(kept, rows, s).astype(BF16)

    left = virt[pl.ds(pl.multiple_of(pl.program_id(1) * part, part), part), :]
    made = []
    for n in range(step):
        right = jnp.concatenate([r[n] for r in refs[:n_split]], axis=0)
        made.append(jnp.dot(left, right, preferred_element_type=F32).astype(BF16))
    out[...] = jnp.swapaxes(jnp.stack(made), 0, 1)


def last_kernel(n_split, n_tensor, scale, g_ref, *refs):
    firsts, out = refs[:n_tensor], refs[n_tensor]
    rows = firsts[0].shape[0]
    naux = g_ref.shape[2]
    group = firsts[0].shape[1] // naux
    width = naux // n_split
    totals = [jnp.zeros((naux, naux), F32) for _ in range(n_split)]
    for k in range(n_tensor):
        left = jnp.concatenate([firsts[k][:, l * naux:(l + 1) * naux] for l in range(group)], axis=0)
        for j in range(n_split):
            start = (k * n_split + j) * group
            right = g_ref[start:start + group].reshape(group * rows, naux)
            totals[j] += lax.dot_general(left, right, (((0,), (0,)), ((), ())), preferred_element_type=F32)
    result = totals[0][:width]
    for j in range(1, n_split):
        result = result + totals[j][j * width:(j + 1) * width]
    out[...] = result * scale


def stages(count):
    bit, found = 1, []
    while bit < count:
        found.append([bit, 2 * bit, 3 * bit] if 2 * bit < count else [bit])
        bit *= 4
    return found


def local(three_centre, green_occ, green_virt, occ_mask, virt_mask, *, n_split, n_tensor):
    rows, cols, naux = three_centre.shape
    nao = green_occ.shape[1]
    packed_width = cols // n_split * naux
    count = n_split * n_tensor
    params = pltpu.CompilerParams(vmem_limit_bytes=VMEM_LIMIT)
    smem = pl.BlockSpec(memory_space=pltpu.SMEM)
    vmem = pl.BlockSpec(memory_space=pltpu.VMEM)
    hbm = pl.BlockSpec(memory_space=pltpu.HBM)

    def exchange(x, split_bits=0, tensor_bits=0):
        bits = split_bits * n_tensor + tensor_bits
        return lax.ppermute(x, ("split", "tensor"), [(d, d ^ bits) for d in range(count)])

    basis, *packed = pl.pallas_call(
        functools.partial(pack_kernel, n_split),
        out_shape=[jax.ShapeDtypeStruct((cols, rows, naux), BF16)]
        + [jax.ShapeDtypeStruct((rows, packed_width + nao), BF16)] * n_split,
        in_specs=[hbm] * 3,
        out_specs=[vmem] * (n_split + 1),
        scratch_shapes=[
            pltpu.SMEM(occ_mask.shape, jnp.int32),
            pltpu.VMEM(three_centre.shape, BF16),
            pltpu.VMEM(green_occ.shape, BF16),
            pltpu.SemaphoreType.DMA((3,)),
        ],
        compiler_params=pltpu.CompilerParams(vmem_limit_bytes=PACK_VMEM_LIMIT),
    )(occ_mask, three_centre, green_occ)
    virt, *packed = lax.optimization_barrier((green_virt, *packed))
    packed = [packed[0]] + [exchange(packed[m], split_bits=m) for m in range(1, n_split)]

    for near in stages(n_tensor):
        virt = jnp.concatenate([virt] + [exchange(virt, tensor_bits=k) for k in near], axis=0)

    virt, *packed = lax.optimization_barrier((virt, *packed))

    firsts = pl.pallas_call(
        functools.partial(first_kernel, n_split, n_tensor, packed_width),
        out_shape=[jax.ShapeDtypeStruct((cols, packed_width), BF16)] * n_tensor,
        in_specs=[vmem] * n_split,
        out_specs=[vmem] * n_tensor,
        compiler_params=params,
    )(*packed)
    basis, *firsts = lax.optimization_barrier((basis, *firsts))

    held = {0: basis}
    bit = n_split // 2
    held[bit] = exchange(basis, split_bits=bit)
    half = n_tensor // 2
    far = [exchange(firsts[k], tensor_bits=k) for k in reversed(range(half, n_tensor))]
    held[bit], *far = lax.optimization_barrier((held[bit], *far))
    near = [exchange(firsts[k], tensor_bits=k) for k in reversed(range(1, half))]
    firsts = [firsts[0], *near[::-1], *far[::-1]]
    while bit > 1:
        bit //= 2
        held.update({m | bit: exchange(x, split_bits=bit) for m, x in held.items()})

    step, part = 16, min(nao, 256)
    g = pl.pallas_call(
        functools.partial(g_kernel, n_split, n_tensor),
        grid=(cols // step, nao // part),
        out_shape=jax.ShapeDtypeStruct((nao, cols, naux), BF16),
        in_specs=[smem, pl.BlockSpec((nao, nao), lambda i, j: (0, 0))]
        + [pl.BlockSpec((step, rows, naux), lambda i, j: (i, 0, 0))] * n_split,
        out_specs=pl.BlockSpec((part, step, naux), lambda i, j: (j, i, 0)),
        scratch_shapes=[pltpu.VMEM((nao, nao), BF16)],
        compiler_params=params,
    )(virt_mask, virt, *[held[m] for m in range(n_split)])

    total = pl.pallas_call(
        functools.partial(last_kernel, n_split, n_tensor, 1.0 / nao),
        out_shape=jax.ShapeDtypeStruct((naux // n_split, naux), F32),
        in_specs=[vmem] * (1 + n_tensor),
        out_specs=vmem,
        compiler_params=params,
    )(g, *firsts)
    for near in stages(n_tensor):
        got = [exchange(total, tensor_bits=k) for k in near]
        for x in got:
            total = total + x
    return total


def solution(mesh):
    sizes = dict(mesh.shape)
    return jax.shard_map(
        functools.partial(local, n_split=sizes["split"], n_tensor=sizes["tensor"]),
        mesh=mesh,
        in_specs=(P("split", "tensor", None), P("split", None), P("tensor", None), P(), P()),
        out_specs=P("split", None),
        check_vma=False,
    )
```

```python
import functools

import jax
import jax.numpy as jnp
from jax import lax
from jax.experimental import pallas as pl
from jax.experimental.pallas import tpu as pltpu
from jax.sharding import PartitionSpec as P

VMEM_LIMIT = 24 * 1024 * 1024
NEAR = 3
BF16 = jnp.bfloat16
F32 = jnp.float32


def xor_blocks(x, width, index):
    cols = x.shape[1]
    bit = 1
    while width * bit < cols:
        span = width * bit
        order = []
        for start in range(0, cols, 2 * span):
            order += [x[:, start + span:start + 2 * span], x[:, start:start + span]]
        x = jnp.where((index & bit) != 0, jnp.concatenate(order, axis=1), x)
        bit *= 2
    return x


def screened(green, mask_ref, first_row, block):
    rows, cols = green.shape
    column = lax.broadcasted_iota(jnp.int32, (1, cols), 1) // block
    parts = []
    for r in range(rows // block):
        keep = jnp.zeros((1, cols), jnp.int32)
        for c in range(cols // block):
            keep = jnp.where(column == c, mask_ref[first_row + r, c], keep)
        part = green[r * block:(r + 1) * block].astype(F32)
        parts.append(jnp.where(keep > 0, part, 0.0))
    return jnp.concatenate(parts, axis=0) if len(parts) > 1 else parts[0]


def swap_lane_blocks(tiles, width):
    tiles = list(tiles)
    count = len(tiles)
    lanes = tiles[0].shape[1]
    lane = lax.broadcasted_iota(jnp.int32, tiles[0].shape, 1)
    half = count // 2
    while half:
        span = half * width
        low = (lane // span) % 2 == 0
        for j in range(count):
            if j & half:
                continue
            a, b = tiles[j], tiles[j | half]
            tiles[j] = jnp.where(low, a, pltpu.roll(b, span, 1))
            tiles[j | half] = jnp.where(low, pltpu.roll(a, lanes - span, 1), b)
        half //= 2
    return tiles


def xor_list(items, index):
    bit = 1
    while bit < len(items):
        flag = (index & bit) != 0
        items = [jnp.where(flag, items[m ^ bit], items[m]) for m in range(len(items))]
        bit *= 2
    return items


def pack_kernel(n_split, occ_mask_hbm, virt_mask_hbm, b_hbm, occ_hbm, virt_hbm, basis_ref, virt_ref, *rest):
    outs, (occ_mask, virt_mask, b, occ_green, virt_green, sems) = rest[:n_split], rest[n_split:]
    pairs = (
        (b_hbm, b), (occ_hbm, occ_green), (virt_hbm, virt_green), (occ_mask_hbm, occ_mask), (virt_mask_hbm, virt_mask)
    )
    copies = [pltpu.make_async_copy(src, dst, sems.at[i]) for i, (src, dst) in enumerate(pairs)]
    for copy in copies:
        copy.start()
    s, t = lax.axis_index("split"), lax.axis_index("tensor")
    rows, cols, naux = b.shape
    group = cols // n_split
    block = occ_green.shape[1] // occ_mask.shape[0]
    for copy in copies[1:]:
        copy.wait()
    virt = screened(virt_green[...], virt_mask, t * (cols // block), block)
    virt_ref[...] = virt.astype(BF16)
    occ = screened(occ_green[...], occ_mask, s * (rows // block), block)
    occ = xor_blocks(occ, cols, t).astype(BF16)
    for m in range(n_split):
        outs[m][:, group * naux:] = occ
    copies[0].wait()
    basis_ref[...] = jnp.swapaxes(b[...], 0, 1)
    for l in range(group):
        tiles = swap_lane_blocks([basis_ref[j * group + l] for j in range(n_split)], naux // n_split)
        tiles = xor_list(tiles, s)
        for m in range(n_split):
            outs[m][:, l * naux:(l + 1) * naux] = tiles[m]


def first_kernel(n_split, n_tensor, width, basis_ref, own_ref, *refs):
    packed, fetched, outs = refs[:n_split], refs[n_split:-n_tensor - 1], refs[-n_tensor - 1:]
    whole = jnp.concatenate([p[...] for p in packed], axis=0)
    first = lax.dot_general(
        whole[:, width:], whole[:, :width], (((0,), (0,)), ((), ())), preferred_element_type=F32
    )
    cols, rows, naux = basis_ref.shape
    for k in range(n_tensor):
        outs[k][...] = first[k * cols:(k + 1) * cols].astype(BF16)
    raw = outs[n_tensor]
    raw[:cols] = basis_ref[...]
    at = cols * rows
    for j, ref in enumerate(fetched):
        block = ref[...]
        if j == 0:
            block = jnp.where(lax.axis_index("split") == 0, own_ref[...], block)
        for c in range(block.shape[1] // naux):
            raw[at // rows, at % rows:at % rows + cols, :] = block[:, c * naux:(c + 1) * naux]
            at += cols


def g_kernel(n_split, n_tensor, *refs):
    raws, out, virt = refs[:n_split], refs[n_split], refs[n_split + 1]
    nao, cols, naux = out.shape
    rows = raws[0].shape[1]
    s = lax.axis_index("split")
    at = cols * rows
    for j in range(n_tensor // n_split):
        for c in range(nao // naux):
            tiles = xor_list([r[at // rows, at % rows:at % rows + cols, :] for r in raws], s)
            for m, tile in enumerate(tiles):
                k = j * n_split + m
                virt[k * cols:(k + 1) * cols, c * naux:(c + 1) * naux] = tile
            at += cols
    virt[...] = xor_blocks(virt[...], rows, s)
    part, step = min(nao, 256), 16

    @pl.loop(0, nao // part)
    def _(i):
        band = pl.ds(pl.multiple_of(i * part, part), part)
        left = virt[band, :]
        for start in range(0, cols, step):
            made = []
            for n in range(start, start + step):
                right = jnp.concatenate([r[n] for r in raws], axis=0)
                made.append(jnp.dot(left, right, preferred_element_type=F32).astype(BF16))
            out[band, start:start + step, :] = jnp.swapaxes(jnp.stack(made), 0, 1)


def last_kernel(n_split, n_tensor, scale, g_ref, *refs):
    firsts, out = refs[:n_tensor], refs[n_tensor]
    rows = firsts[0].shape[0]
    naux = g_ref.shape[2]
    group = firsts[0].shape[1] // naux
    width = naux // n_split
    totals = [jnp.zeros((naux, naux), F32) for _ in range(n_split)]
    for k in range(n_tensor):
        left = jnp.concatenate([firsts[k][:, l * naux:(l + 1) * naux] for l in range(group)], axis=0)
        for j in range(n_split):
            start = (k * n_split + j) * group
            right = g_ref[start:start + group].reshape(group * rows, naux)
            totals[j] += lax.dot_general(left, right, (((0,), (0,)), ((), ())), preferred_element_type=F32)
    result = totals[0][:width]
    for j in range(1, n_split):
        result = result + totals[j][j * width:(j + 1) * width]
    out[...] = result * scale


def stages(count):
    bit, found = 1, []
    while bit < count:
        found.append([bit, 2 * bit, 3 * bit] if 2 * bit < count else [bit])
        bit *= 4
    return found


def local(three_centre, green_occ, green_virt, occ_mask, virt_mask, *, n_split, n_tensor):
    rows, cols, naux = three_centre.shape
    nao = green_occ.shape[1]
    packed_width = cols // n_split * naux
    count = n_split * n_tensor
    params = pltpu.CompilerParams(vmem_limit_bytes=VMEM_LIMIT)
    vmem = pl.BlockSpec(memory_space=pltpu.VMEM)
    hbm = pl.BlockSpec(memory_space=pltpu.HBM)

    def exchange(x, split_bits=0, tensor_bits=0):
        bits = split_bits * n_tensor + tensor_bits
        return lax.ppermute(x, ("split", "tensor"), [(d, d ^ bits) for d in range(count)])

    def fetch(x, j):
        pairs = [(s * n_tensor + t, s * n_tensor + (t ^ (j * n_split + s))) for s in range(n_split) for t in range(n_tensor)]
        return lax.ppermute(x, ("split", "tensor"), [(a, b) for a, b in pairs if a != b])

    arguments = [occ_mask, virt_mask, three_centre, green_occ, green_virt]
    basis, virt, *packed = pl.pallas_call(
        functools.partial(pack_kernel, n_split),
        out_shape=[jax.ShapeDtypeStruct((cols, rows, naux), BF16), jax.ShapeDtypeStruct(green_virt.shape, BF16)]
        + [jax.ShapeDtypeStruct((rows, packed_width + nao), BF16)] * n_split,
        in_specs=[hbm] * 5,
        out_specs=[vmem] * (n_split + 2),
        scratch_shapes=[
            pltpu.SMEM(occ_mask.shape, jnp.int32),
            pltpu.SMEM(virt_mask.shape, jnp.int32),
            pltpu.VMEM(three_centre.shape, BF16),
            pltpu.VMEM(green_occ.shape, BF16),
            pltpu.VMEM(green_virt.shape, BF16),
            pltpu.SemaphoreType.DMA((5,)),
        ],
        compiler_params=params,
    )(*[pltpu.with_memory_space_constraint(x, pltpu.HBM) for x in arguments])
    packed = [packed[0]] + [exchange(packed[m], split_bits=m) for m in range(1, n_split)]

    own = virt
    virt, packed[1] = lax.optimization_barrier((virt, packed[1]))
    fetched = [fetch(virt, j) for j in range(n_tensor // n_split)]

    slots = n_tensor // n_split * nao // rows * cols // naux
    *firsts, raw = pl.pallas_call(
        functools.partial(first_kernel, n_split, n_tensor, packed_width),
        out_shape=[jax.ShapeDtypeStruct((cols, packed_width), BF16)] * n_tensor
        + [jax.ShapeDtypeStruct((cols + slots, rows, naux), BF16)],
        in_specs=[vmem] * (2 + n_split + len(fetched)),
        out_specs=[vmem] * (n_tensor + 1),
        compiler_params=params,
    )(basis, own, *packed, *fetched)

    held = {0: raw}
    bit = n_split // 2
    held[bit] = exchange(raw, split_bits=bit)
    got = {0: firsts[0]}
    got.update({k: exchange(firsts[k], tensor_bits=k) for k in range(n_tensor - 1, 0, -1)})
    together = range(NEAR, n_tensor)
    held[bit], *tied = lax.optimization_barrier((held[bit], *[got[k] for k in together]))
    got.update(zip(together, tied))
    while bit > 1:
        bit //= 2
        held.update({m | bit: exchange(x, split_bits=bit) for m, x in held.items()})

    g = pl.pallas_call(
        functools.partial(g_kernel, n_split, n_tensor),
        out_shape=jax.ShapeDtypeStruct((nao, cols, naux), BF16),
        in_specs=[vmem] * n_split,
        out_specs=vmem,
        scratch_shapes=[pltpu.VMEM((nao, nao), BF16)],
        compiler_params=params,
    )(*[held[m] for m in range(n_split)])

    total = pl.pallas_call(
        functools.partial(last_kernel, n_split, n_tensor, 1.0 / nao),
        out_shape=jax.ShapeDtypeStruct((naux // n_split, naux), F32),
        in_specs=[vmem] * (1 + n_tensor),
        out_specs=vmem,
        compiler_params=params,
    )(g, *[got[k] for k in range(n_tensor)])
    for near in stages(n_tensor):
        got = [exchange(total, tensor_bits=k) for k in near]
        for x in got:
            total = total + x
    return total


def solution(mesh):
    sizes = dict(mesh.shape)
    return jax.shard_map(
        functools.partial(local, n_split=sizes["split"], n_tensor=sizes["tensor"]),
        mesh=mesh,
        in_specs=(P("split", "tensor", None), P("split", None), P("tensor", None), P(), P()),
        out_specs=P("split", None),
        check_vma=False,
    )
```

```python
import functools

import jax
import jax.numpy as jnp
from jax import lax
from jax.experimental import pallas as pl
from jax.experimental.pallas import tpu as pltpu
from jax.sharding import PartitionSpec as P

VMEM_LIMIT = 40 * 1024 * 1024
BF16 = jnp.bfloat16
F32 = jnp.float32


def xor_blocks(x, width, index):
    cols = x.shape[1]
    bit = 1
    while width * bit < cols:
        span = width * bit
        order = []
        for start in range(0, cols, 2 * span):
            order += [x[:, start + span:start + 2 * span], x[:, start:start + span]]
        x = jnp.where((index & bit) != 0, jnp.concatenate(order, axis=1), x)
        bit *= 2
    return x


def screened(green, mask_ref, first_row, block):
    rows, cols = green.shape
    column = lax.broadcasted_iota(jnp.int32, (1, cols), 1) // block
    parts = []
    for r in range(rows // block):
        keep = jnp.zeros((1, cols), jnp.int32)
        for c in range(cols // block):
            keep = jnp.where(column == c, mask_ref[first_row + r, c], keep)
        part = green[r * block:(r + 1) * block].astype(F32)
        parts.append(jnp.where(keep > 0, part, 0.0))
    return jnp.concatenate(parts, axis=0) if len(parts) > 1 else parts[0]


def swap_lane_blocks(tiles, width):
    tiles = list(tiles)
    count = len(tiles)
    lanes = tiles[0].shape[1]
    lane = lax.broadcasted_iota(jnp.int32, tiles[0].shape, 1)
    half = count // 2
    while half:
        span = half * width
        low = (lane // span) % 2 == 0
        for j in range(count):
            if j & half:
                continue
            a, b = tiles[j], tiles[j | half]
            tiles[j] = jnp.where(low, a, pltpu.roll(b, span, 1))
            tiles[j | half] = jnp.where(low, pltpu.roll(a, lanes - span, 1), b)
        half //= 2
    return tiles


def xor_list(items, index):
    bit = 1
    while bit < len(items):
        flag = (index & bit) != 0
        items = [jnp.where(flag, items[m ^ bit], items[m]) for m in range(len(items))]
        bit *= 2
    return items


def pack_kernel(n_split, occ_mask_hbm, virt_mask_hbm, b_hbm, occ_hbm, virt_hbm, virt_ref, *rest):
    outs, (occ_mask, virt_mask, b, occ_green, virt_green, sems) = rest[:n_split], rest[n_split:]
    pairs = (
        (b_hbm, b), (occ_hbm, occ_green), (virt_hbm, virt_green), (occ_mask_hbm, occ_mask), (virt_mask_hbm, virt_mask)
    )
    copies = [pltpu.make_async_copy(src, dst, sems.at[i]) for i, (src, dst) in enumerate(pairs)]
    for copy in copies:
        copy.start()
    s, t = lax.axis_index("split"), lax.axis_index("tensor")
    rows, cols, naux = b.shape
    group = cols // n_split
    block = occ_green.shape[1] // occ_mask.shape[0]
    for copy in copies[1:]:
        copy.wait()
    virt = screened(virt_green[...], virt_mask, t * (cols // block), block)
    virt_ref[...] = virt.astype(BF16)
    occ = screened(occ_green[...], occ_mask, s * (rows // block), block)
    occ = xor_blocks(occ, cols, t).astype(BF16)
    for m in range(n_split):
        outs[m][:, group * naux:] = occ
    copies[0].wait()
    basis = jnp.swapaxes(b[...], 0, 1)
    for l in range(group):
        tiles = swap_lane_blocks([basis[j * group + l] for j in range(n_split)], naux // n_split)
        tiles = xor_list(tiles, s)
        for m in range(n_split):
            outs[m][:, l * naux:(l + 1) * naux] = tiles[m]


def others(n_split, m):
    return [i for i in range(n_split) if i // 2 != m // 2]


def write_rows(out, start, blocks):
    rows, at = out.shape[0], 0
    for block in blocks:
        height = block.shape[0]
        for c in range(0, block.shape[1], 128):
            column = start + at // rows * 128
            out[at % rows:at % rows + height, column:column + 128] = block[:, c:c + 128]
            at += height


def read_rows(ref, start, count, height, width):
    rows, at, blocks = ref.shape[0], 0, []
    for _ in range(count):
        tiles = []
        for c in range(0, width, 128):
            column = start + at // rows * 128
            tiles.append(ref[at % rows:at % rows + height, column:column + 128])
            at += height
        blocks.append(jnp.concatenate(tiles, axis=1))
    return blocks


def first_kernel(n_split, n_tensor, width, own_virt, *refs):
    own, got, rest = refs[:n_split], refs[n_split:2 * n_split - 1], refs[2 * n_split - 1:]
    shares = n_tensor // n_split
    fetched, firsts, raws = rest[:shares], rest[shares:shares + n_tensor], rest[shares + n_tensor:]
    whole = jnp.concatenate([p[...] for p in (own[0], *got)], axis=0)
    first = lax.dot_general(
        whole[:, width:], whole[:, :width], (((0,), (0,)), ((), ())), preferred_element_type=F32
    )
    cols = first.shape[0] // n_tensor
    for k in range(n_tensor):
        firsts[k][...] = first[k * cols:(k + 1) * cols].astype(BF16)
    blocks = [f[...] for f in fetched]
    blocks[0] = jnp.where(lax.axis_index("split") == 0, own_virt[...], blocks[0])
    for p in range(1, n_split // 2):
        for n, i in enumerate(others(n_split, 2 * p)):
            raws[p - 1][:, n * width:(n + 1) * width] = own[i][:, :width]
        write_rows(raws[p - 1], (n_split - 2) * width, blocks)
    pieces = [own[i] for i in range(n_split) if i != 1] + list(got[1:])
    for n, piece in enumerate(pieces):
        raws[-1][:, n * width:(n + 1) * width] = piece[:, :width]
    write_rows(raws[-1], len(pieces) * width, blocks)


def g_kernel(n_split, n_tensor, width, *refs):
    own, got, refs = refs[:n_split], refs[n_split:2 * n_split - 1], refs[2 * n_split - 1:]
    raws, core, own_core, out, virt = refs[:n_split - 2], *refs[n_split - 2:]
    cols, nao, naux = out.shape
    rows = core.shape[0]
    group = cols // n_split
    shares = n_tensor // n_split
    s = lax.axis_index("split")

    def piece(m, q):
        if m == 0:
            return own[q], 0
        if q == 0:
            return got[m - 1], 0
        if m == 1:
            return core, [i for i in range(n_split) if i != 1].index(q ^ 1)
        if q == 1:
            return core, n_split - 1 + (m ^ 1) - 2
        return raws[m - 2], others(n_split, m).index(m ^ q)

    core_start = (2 * n_split - 3) * width
    found = [read_rows(own_core, core_start, shares, cols, nao), read_rows(core, core_start, shares, cols, nao)]
    found += [read_rows(r, (n_split - 2) * width, shares, cols, nao) for r in raws]
    blocks = [tile for i in range(shares) for tile in xor_list([f[i] for f in found], s)]
    ordered = xor_blocks(jnp.concatenate(blocks, axis=0), rows, s)
    row = lax.broadcasted_iota(jnp.int32, (nao, nao), 0)
    column = lax.broadcasted_iota(jnp.int32, (nao, nao), 1)
    j, k, l = row // (n_tensor * group), row // group % n_tensor, row % group
    place = jnp.where(column == k * cols + j * group + l, 1.0, 0.0).astype(BF16)
    virt[...] = jnp.dot(place, ordered, preferred_element_type=F32).astype(BF16)
    part = min(nao, 256)

    @pl.loop(0, nao // part)
    def _(i):
        band = pl.ds(pl.multiple_of(i * part, part), part)
        left = virt[band, :]
        for l in range(group):
            right = []
            for q in range(n_split):
                tiles = []
                for m in range(n_split):
                    ref, n = piece(m, q)
                    tiles.append(ref[:, n * width + l * naux:n * width + (l + 1) * naux])
                right.append(jnp.concatenate(tiles, axis=0))
            made = jnp.dot(left, jnp.concatenate(right, axis=1), preferred_element_type=F32).astype(BF16)
            tiles = swap_lane_blocks([made[:, q * naux:(q + 1) * naux] for q in range(n_split)], naux // n_split)
            for j, tile in enumerate(tiles):
                out[j * group + l, band, :] = tile


def last_kernel(n_split, n_tensor, scale, g_ref, *refs):
    firsts, out = refs[:n_tensor][::-1], refs[n_tensor]
    naux = g_ref.shape[2]
    group = firsts[0].shape[1] // naux
    width = naux // n_split
    depth = n_tensor * group
    left = jnp.stack([f[:, l * naux:(l + 1) * naux] for f in firsts for l in range(group)])
    left = jnp.swapaxes(left, 0, 1).reshape(-1, naux)
    right = [g_ref[:, j * depth:(j + 1) * depth, :].reshape(-1, naux) for j in range(n_split)]
    total = lax.dot_general(
        left, jnp.concatenate(right, axis=1), (((0,), (0,)), ((), ())), preferred_element_type=F32
    )
    result = total[:width, :naux]
    for j in range(1, n_split):
        result = result + total[j * width:(j + 1) * width, j * naux:(j + 1) * naux]
    out[...] = xor_blocks(result * scale, width, lax.axis_index("split"))


def stages(count):
    bit, found = 1, []
    while bit < count:
        found.append([bit, 2 * bit, 3 * bit] if 2 * bit < count else [bit])
        bit *= 4
    return found


def local(three_centre, green_occ, green_virt, occ_mask, virt_mask, *, n_split, n_tensor):
    rows, cols, naux = three_centre.shape
    nao = green_occ.shape[1]
    packed_width = cols // n_split * naux
    count = n_split * n_tensor
    params = pltpu.CompilerParams(vmem_limit_bytes=VMEM_LIMIT)
    vmem = pl.BlockSpec(memory_space=pltpu.VMEM)
    hbm = pl.BlockSpec(memory_space=pltpu.HBM)

    def exchange(x, split_bits=0, tensor_bits=0):
        bits = split_bits * n_tensor + tensor_bits
        return lax.ppermute(x, ("split", "tensor"), [(d, d ^ bits) for d in range(count)])

    def fetch(x, j):
        pairs = [(s * n_tensor + t, s * n_tensor + (t ^ (j * n_split + s))) for s in range(n_split) for t in range(n_tensor)]
        return lax.ppermute(x, ("split", "tensor"), [(a, b) for a, b in pairs if a != b])

    arguments = [occ_mask, virt_mask, three_centre, green_occ, green_virt]
    virt, *packed = pl.pallas_call(
        functools.partial(pack_kernel, n_split),
        out_shape=[jax.ShapeDtypeStruct(green_virt.shape, BF16)]
        + [jax.ShapeDtypeStruct((rows, packed_width + nao), BF16)] * n_split,
        in_specs=[hbm] * 5,
        out_specs=[vmem] * (n_split + 1),
        scratch_shapes=[
            pltpu.SMEM(occ_mask.shape, jnp.int32),
            pltpu.SMEM(virt_mask.shape, jnp.int32),
            pltpu.VMEM(three_centre.shape, BF16),
            pltpu.VMEM(green_occ.shape, BF16),
            pltpu.VMEM(green_virt.shape, BF16),
            pltpu.SemaphoreType.DMA((5,)),
        ],
        compiler_params=params,
    )(*[pltpu.with_memory_space_constraint(x, pltpu.HBM) for x in arguments])
    received = [exchange(packed[m], split_bits=m) for m in range(1, n_split)]

    own = virt
    virt, received[0] = lax.optimization_barrier((virt, received[0]))
    shares = n_tensor // n_split
    fetched = [fetch(virt, j) for j in range(shares)]

    virt_width = shares * nao * cols // rows
    widths = [(n_split - 2) * packed_width + virt_width] * (n_split // 2 - 1) + [(2 * n_split - 3) * packed_width + virt_width]
    made = pl.pallas_call(
        functools.partial(first_kernel, n_split, n_tensor, packed_width),
        out_shape=[jax.ShapeDtypeStruct((cols, packed_width), BF16)] * n_tensor
        + [jax.ShapeDtypeStruct((rows, w), BF16) for w in widths],
        in_specs=[vmem] * (2 * n_split + shares),
        out_specs=[vmem] * (n_tensor + len(widths)),
        compiler_params=params,
    )(own, *packed, *received, *fetched)
    firsts, raws = made[:n_tensor], made[n_tensor:]

    moved = {}
    moved.update({m: exchange(raws[m // 2 - 1], split_bits=m) for m in range(2, n_split, 2)})
    got = {0: firsts[0]}
    ahead = [n_tensor - 1, n_tensor - 2]
    got.update({k: exchange(firsts[k], tensor_bits=k) for k in ahead})
    later = [k for k in range(n_tensor - 1, 0, -1) if k not in ahead]
    evens = list(range(2, n_split, 2))
    tied = list(lax.optimization_barrier((*[got[k] for k in ahead], *[moved[m] for m in evens], raws[-1], *[firsts[k] for k in later])))
    got.update(zip(ahead, tied))
    moved.update(zip(evens, tied[len(ahead):]))
    moved[1] = exchange(tied.pop(len(ahead) + len(evens)), split_bits=1)
    firsts = dict(enumerate(firsts))
    firsts.update(zip(later, tied[len(ahead) + len(evens):]))
    got.update({k: exchange(firsts[k], tensor_bits=k) for k in later})
    got = [got[k] for k in range(n_tensor)]
    moved.update({m + 1: exchange(moved[m], split_bits=1) for m in range(2, n_split, 2)})
    moved = [moved[m] for m in range(2, n_split)] + [moved[1]]

    g = pl.pallas_call(
        functools.partial(g_kernel, n_split, n_tensor, packed_width),
        out_shape=jax.ShapeDtypeStruct((cols, nao, naux), BF16),
        in_specs=[vmem] * (3 * n_split - 1),
        out_specs=vmem,
        scratch_shapes=[pltpu.VMEM((nao, nao), BF16)],
        compiler_params=params,
    )(*packed, *received, *moved, raws[-1])

    total = pl.pallas_call(
        functools.partial(last_kernel, n_split, n_tensor, 1.0 / nao),
        out_shape=jax.ShapeDtypeStruct((naux // n_split, naux), F32),
        in_specs=[vmem] * (1 + n_tensor),
        out_specs=vmem,
        compiler_params=params,
    )(g, *got[::-1])
    for near in stages(n_tensor):
        got = [exchange(total, tensor_bits=k) for k in near]
        for x in got:
            total = total + x
    return total


def solution(mesh):
    sizes = dict(mesh.shape)
    return jax.shard_map(
        functools.partial(local, n_split=sizes["split"], n_tensor=sizes["tensor"]),
        mesh=mesh,
        in_specs=(P("split", "tensor", None), P("split", None), P("tensor", None), P(), P()),
        out_specs=P("split", None),
        check_vma=False,
    )
```

```python
import functools

import jax
import jax.numpy as jnp
from jax import lax
from jax.experimental import pallas as pl
from jax.experimental.pallas import tpu as pltpu
from jax.sharding import PartitionSpec as P

VMEM_LIMIT = 40 * 1024 * 1024
BF16 = jnp.bfloat16
F32 = jnp.float32


def xor_blocks(x, width, index):
    cols = x.shape[1]
    bit = 1
    while width * bit < cols:
        span = width * bit
        order = []
        for start in range(0, cols, 2 * span):
            order += [x[:, start + span:start + 2 * span], x[:, start:start + span]]
        x = jnp.where((index & bit) != 0, jnp.concatenate(order, axis=1), x)
        bit *= 2
    return x


def screened(green, mask_ref, first_row, block):
    rows, cols = green.shape
    column = lax.broadcasted_iota(jnp.int32, (1, cols), 1) // block
    parts = []
    for r in range(rows // block):
        keep = jnp.zeros((1, cols), jnp.int32)
        for c in range(cols // block):
            keep = jnp.where(column == c, mask_ref[first_row + r, c], keep)
        part = green[r * block:(r + 1) * block].astype(F32)
        parts.append(jnp.where(keep > 0, part, 0.0))
    return jnp.concatenate(parts, axis=0) if len(parts) > 1 else parts[0]


def swap_lane_blocks(tiles, width):
    tiles = list(tiles)
    count = len(tiles)
    lanes = tiles[0].shape[1]
    lane = lax.broadcasted_iota(jnp.int32, tiles[0].shape, 1)
    half = count // 2
    while half:
        span = half * width
        low = (lane // span) % 2 == 0
        for j in range(count):
            if j & half:
                continue
            a, b = tiles[j], tiles[j | half]
            tiles[j] = jnp.where(low, a, pltpu.roll(b, span, 1))
            tiles[j | half] = jnp.where(low, pltpu.roll(a, lanes - span, 1), b)
        half //= 2
    return tiles


def xor_list(items, index):
    bit = 1
    while bit < len(items):
        flag = (index & bit) != 0
        items = [jnp.where(flag, items[m ^ bit], items[m]) for m in range(len(items))]
        bit *= 2
    return items


def pack_kernel(n_split, occ_mask_hbm, virt_mask_hbm, b_hbm, occ_hbm, virt_hbm, virt_ref, *rest):
    outs, (occ_mask, virt_mask, b, occ_green, virt_green, sems) = rest[:n_split], rest[n_split:]
    pairs = (
        (b_hbm, b), (occ_hbm, occ_green), (virt_hbm, virt_green), (occ_mask_hbm, occ_mask), (virt_mask_hbm, virt_mask)
    )
    copies = [pltpu.make_async_copy(src, dst, sems.at[i]) for i, (src, dst) in enumerate(pairs)]
    for copy in copies:
        copy.start()
    s, t = lax.axis_index("split"), lax.axis_index("tensor")
    rows, cols, naux = b.shape
    group = cols // n_split
    block = occ_green.shape[1] // occ_mask.shape[0]
    for copy in copies[1:]:
        copy.wait()
    virt = screened(virt_green[...], virt_mask, t * (cols // block), block)
    virt_ref[...] = virt.astype(BF16)
    occ = screened(occ_green[...], occ_mask, s * (rows // block), block)
    occ = xor_blocks(occ, cols, t).astype(BF16)
    for m in range(n_split):
        outs[m][:, group * naux:] = occ
    copies[0].wait()
    basis = jnp.swapaxes(b[...], 0, 1)
    for l in range(group):
        tiles = swap_lane_blocks([basis[j * group + l] for j in range(n_split)], naux // n_split)
        tiles = xor_list(tiles, s)
        for m in range(n_split):
            outs[m][:, l * naux:(l + 1) * naux] = tiles[m]


def add_kernel(*refs):
    refs[-1][...] = sum(r[...] for r in refs[:-1])


def others(n_split, m):
    return [i for i in range(n_split) if i // 2 != m // 2]


def write_rows(out, start, blocks):
    rows, at = out.shape[0], 0
    for block in blocks:
        height = block.shape[0]
        for c in range(0, block.shape[1], 128):
            column = start + at // rows * 128
            out[at % rows:at % rows + height, column:column + 128] = block[:, c:c + 128]
            at += height


def read_rows(ref, start, count, height, width):
    rows, at, blocks = ref.shape[0], 0, []
    for _ in range(count):
        tiles = []
        for c in range(0, width, 128):
            column = start + at // rows * 128
            tiles.append(ref[at % rows:at % rows + height, column:column + 128])
            at += height
        blocks.append(jnp.concatenate(tiles, axis=1))
    return blocks


def first_kernel(n_split, n_tensor, width, own_virt, *refs):
    own, got, rest = refs[:n_split], refs[n_split:2 * n_split - 1][::-1], refs[2 * n_split - 1:]
    shares = n_tensor // n_split
    fetched, firsts, raws = rest[:shares], rest[shares:shares + n_tensor], rest[shares + n_tensor:]
    whole = jnp.concatenate([p[...] for p in (own[0], *got)], axis=0)
    first = lax.dot_general(
        whole[:, width:], whole[:, :width], (((0,), (0,)), ((), ())), preferred_element_type=F32
    )
    cols = first.shape[0] // n_tensor
    for k in range(n_tensor):
        firsts[k][...] = first[k * cols:(k + 1) * cols].astype(BF16)
    blocks = [f[...] for f in fetched]
    blocks[0] = jnp.where(lax.axis_index("split") == 0, own_virt[...], blocks[0])
    for p in range(1, n_split // 2):
        for n, i in enumerate(others(n_split, 2 * p)):
            raws[p - 1][:, n * width:(n + 1) * width] = own[i][:, :width]
        write_rows(raws[p - 1], (n_split - 2) * width, blocks)
    pieces = [own[i] for i in range(n_split) if i != 1] + list(got[1:])
    for n, piece in enumerate(pieces):
        raws[-1][:, n * width:(n + 1) * width] = piece[:, :width]
    write_rows(raws[-1], len(pieces) * width, blocks)


def g_kernel(n_split, n_tensor, width, *refs):
    own, got, refs = refs[:n_split], refs[n_split:2 * n_split - 1], refs[2 * n_split - 1:]
    raws, core, own_core, out, virt = refs[:n_split - 2], *refs[n_split - 2:]
    cols, nao, naux = out.shape
    rows = core.shape[0]
    group = cols // n_split
    shares = n_tensor // n_split
    s = lax.axis_index("split")

    def piece(m, q):
        if m == 0:
            return own[q], 0
        if q == 0:
            return got[m - 1], 0
        if m == 1:
            return core, [i for i in range(n_split) if i != 1].index(q ^ 1)
        if q == 1:
            return core, n_split - 1 + (m ^ 1) - 2
        return raws[m - 2], others(n_split, m).index(m ^ q)

    core_start = (2 * n_split - 3) * width
    found = [read_rows(own_core, core_start, shares, cols, nao), read_rows(core, core_start, shares, cols, nao)]
    found += [read_rows(r, (n_split - 2) * width, shares, cols, nao) for r in raws]
    blocks = [tile for i in range(shares) for tile in xor_list([f[i] for f in found], s)]
    ordered = xor_blocks(jnp.concatenate(blocks, axis=0), rows, s)
    row = lax.broadcasted_iota(jnp.int32, (nao, nao), 0)
    column = lax.broadcasted_iota(jnp.int32, (nao, nao), 1)
    j, k, l = row // (n_tensor * group), row // group % n_tensor, row % group
    place = jnp.where(column == k * cols + j * group + l, 1.0, 0.0).astype(BF16)
    virt[...] = jnp.dot(place, ordered, preferred_element_type=F32).astype(BF16)
    part = min(nao, 256)

    @pl.loop(0, nao // part)
    def _(i):
        band = pl.ds(pl.multiple_of(i * part, part), part)
        left = virt[band, :]
        for l in range(group):
            right = []
            for q in range(n_split):
                tiles = []
                for m in range(n_split):
                    ref, n = piece(m, q)
                    tiles.append(ref[:, n * width + l * naux:n * width + (l + 1) * naux])
                right.append(jnp.concatenate(tiles, axis=0))
            made = jnp.dot(left, jnp.concatenate(right, axis=1), preferred_element_type=F32).astype(BF16)
            tiles = swap_lane_blocks([made[:, q * naux:(q + 1) * naux] for q in range(n_split)], naux // n_split)
            for j, tile in enumerate(tiles):
                out[j * group + l, band, :] = tile


def last_kernel(n_split, n_tensor, scale, g_ref, *refs):
    firsts, out = refs[:n_tensor][::-1], refs[n_tensor]
    naux = g_ref.shape[2]
    group = firsts[0].shape[1] // naux
    width = naux // n_split
    depth = n_tensor * group
    left = jnp.stack([f[:, l * naux:(l + 1) * naux] for f in firsts for l in range(group)])
    left = jnp.swapaxes(left, 0, 1).reshape(-1, naux)
    right = [g_ref[:, j * depth:(j + 1) * depth, :].reshape(-1, naux) for j in range(n_split)]
    total = lax.dot_general(
        left, jnp.concatenate(right, axis=1), (((0,), (0,)), ((), ())), preferred_element_type=F32
    )
    result = total[:width, :naux]
    for j in range(1, n_split):
        result = result + total[j * width:(j + 1) * width, j * naux:(j + 1) * naux]
    out[...] = xor_blocks(result * scale, width, lax.axis_index("split"))


def stages(count):
    bit, found = 1, []
    while bit < count:
        found.append([bit, 2 * bit, 3 * bit] if 2 * bit < count else [bit])
        bit *= 4
    return found


def local(three_centre, green_occ, green_virt, occ_mask, virt_mask, *, n_split, n_tensor):
    rows, cols, naux = three_centre.shape
    nao = green_occ.shape[1]
    packed_width = cols // n_split * naux
    count = n_split * n_tensor
    params = pltpu.CompilerParams(vmem_limit_bytes=VMEM_LIMIT)
    vmem = pl.BlockSpec(memory_space=pltpu.VMEM)
    hbm = pl.BlockSpec(memory_space=pltpu.HBM)

    def exchange(x, split_bits=0, tensor_bits=0):
        bits = split_bits * n_tensor + tensor_bits
        return lax.ppermute(x, ("split", "tensor"), [(d, d ^ bits) for d in range(count)])

    def fetch(x, j):
        pairs = [(s * n_tensor + t, s * n_tensor + (t ^ (j * n_split + s))) for s in range(n_split) for t in range(n_tensor)]
        return lax.ppermute(x, ("split", "tensor"), [(a, b) for a, b in pairs if a != b])

    arguments = [occ_mask, virt_mask, three_centre, green_occ, green_virt]
    virt, *packed = pl.pallas_call(
        functools.partial(pack_kernel, n_split),
        out_shape=[jax.ShapeDtypeStruct(green_virt.shape, BF16)]
        + [jax.ShapeDtypeStruct((rows, packed_width + nao), BF16)] * n_split,
        in_specs=[hbm] * 5,
        out_specs=[vmem] * (n_split + 1),
        scratch_shapes=[
            pltpu.SMEM(occ_mask.shape, jnp.int32),
            pltpu.SMEM(virt_mask.shape, jnp.int32),
            pltpu.VMEM(three_centre.shape, BF16),
            pltpu.VMEM(green_occ.shape, BF16),
            pltpu.VMEM(green_virt.shape, BF16),
            pltpu.SemaphoreType.DMA((5,)),
        ],
        compiler_params=params,
    )(*[pltpu.with_memory_space_constraint(x, pltpu.HBM) for x in arguments])
    received = [exchange(packed[m], split_bits=m) for m in range(1, n_split)]

    own = virt
    shares = n_tensor // n_split
    fetched = [fetch(virt, j) for j in range(shares)]

    virt_width = shares * nao * cols // rows
    widths = [(n_split - 2) * packed_width + virt_width] * (n_split // 2 - 1) + [(2 * n_split - 3) * packed_width + virt_width]
    made = pl.pallas_call(
        functools.partial(first_kernel, n_split, n_tensor, packed_width),
        out_shape=[jax.ShapeDtypeStruct((cols, packed_width), BF16)] * n_tensor
        + [jax.ShapeDtypeStruct((rows, w), BF16) for w in widths],
        in_specs=[vmem] * (2 * n_split + shares),
        out_specs=[vmem] * (n_tensor + len(widths)),
        compiler_params=params,
    )(own, *packed, *received[::-1], *fetched)
    firsts, raws = made[:n_tensor], made[n_tensor:]

    moved = {}
    moved.update({m: exchange(raws[m // 2 - 1], split_bits=m) for m in range(2, n_split, 2)})
    got = {0: firsts[0]}
    ahead = [k for k in range(n_tensor - 1, 1, -1) if k != n_tensor // 2]
    got.update({k: exchange(firsts[k], tensor_bits=k) for k in ahead})
    later = [k for k in range(n_tensor - 1, 0, -1) if k not in ahead]
    evens = list(range(2, n_split, 2))
    tied = list(lax.optimization_barrier((*[got[k] for k in ahead], *[moved[m] for m in evens], raws[-1], *[firsts[k] for k in later])))
    got.update(zip(ahead, tied))
    moved.update(zip(evens, tied[len(ahead):]))
    moved[1] = exchange(tied.pop(len(ahead) + len(evens)), split_bits=1)
    firsts = dict(enumerate(firsts))
    firsts.update(zip(later, tied[len(ahead) + len(evens):]))
    got.update({k: exchange(firsts[k], tensor_bits=k) for k in later})
    got = [got[k] for k in range(n_tensor)]
    moved.update({m + 1: exchange(moved[m], split_bits=1) for m in range(2, n_split, 2)})
    moved = [moved[m] for m in range(2, n_split)] + [moved[1]]

    g = pl.pallas_call(
        functools.partial(g_kernel, n_split, n_tensor, packed_width),
        out_shape=jax.ShapeDtypeStruct((cols, nao, naux), BF16),
        in_specs=[vmem] * (3 * n_split - 1),
        out_specs=vmem,
        scratch_shapes=[pltpu.VMEM((nao, nao), BF16)],
        compiler_params=params,
    )(*packed, *received, *moved, raws[-1])

    total = pl.pallas_call(
        functools.partial(last_kernel, n_split, n_tensor, 1.0 / nao),
        out_shape=jax.ShapeDtypeStruct((naux // n_split, naux), F32),
        in_specs=[vmem] * (1 + n_tensor),
        out_specs=vmem,
        compiler_params=params,
    )(g, *got[::-1])
    for near in stages(n_tensor):
        got = [exchange(total, tensor_bits=k) for k in near]
        if near[-1] * 2 < n_tensor:
            total = pl.pallas_call(
                add_kernel,
                out_shape=jax.ShapeDtypeStruct(total.shape, F32),
                in_specs=[vmem] * (1 + len(got)),
                out_specs=vmem,
                compiler_params=params,
            )(total, *got)
        else:
            total = sum(got, total)
    return total


def solution(mesh):
    sizes = dict(mesh.shape)
    return jax.shard_map(
        functools.partial(local, n_split=sizes["split"], n_tensor=sizes["tensor"]),
        mesh=mesh,
        in_specs=(P("split", "tensor", None), P("split", None), P("tensor", None), P(), P()),
        out_specs=P("split", None),
        check_vma=False,
    )
```

```python
import functools

import jax
import jax.numpy as jnp
from jax import lax
from jax.experimental import pallas as pl
from jax.experimental.pallas import tpu as pltpu
from jax.sharding import PartitionSpec as P

VMEM_LIMIT = 40 * 1024 * 1024
BF16 = jnp.bfloat16
F32 = jnp.float32


def xor_blocks(x, width, index):
    cols = x.shape[1]
    bit = 1
    while width * bit < cols:
        span = width * bit
        order = []
        for start in range(0, cols, 2 * span):
            order += [x[:, start + span:start + 2 * span], x[:, start:start + span]]
        x = jnp.where((index & bit) != 0, jnp.concatenate(order, axis=1), x)
        bit *= 2
    return x


def screened(green, mask_ref, first_row, block):
    rows, cols = green.shape
    column = lax.broadcasted_iota(jnp.int32, (1, cols), 1) // block
    parts = []
    for r in range(rows // block):
        keep = jnp.zeros((1, cols), jnp.int32)
        for c in range(cols // block):
            keep = jnp.where(column == c, mask_ref[first_row + r, c], keep)
        part = green[r * block:(r + 1) * block].astype(F32)
        parts.append(jnp.where(keep > 0, part, 0.0))
    return jnp.concatenate(parts, axis=0) if len(parts) > 1 else parts[0]


def swap_lane_blocks(tiles, width):
    tiles = list(tiles)
    count = len(tiles)
    lanes = tiles[0].shape[1]
    lane = lax.broadcasted_iota(jnp.int32, tiles[0].shape, 1)
    half = count // 2
    while half:
        span = half * width
        low = (lane // span) % 2 == 0
        for j in range(count):
            if j & half:
                continue
            a, b = tiles[j], tiles[j | half]
            tiles[j] = jnp.where(low, a, pltpu.roll(b, span, 1))
            tiles[j | half] = jnp.where(low, pltpu.roll(a, lanes - span, 1), b)
        half //= 2
    return tiles


def xor_list(items, index):
    bit = 1
    while bit < len(items):
        flag = (index & bit) != 0
        items = [jnp.where(flag, items[m ^ bit], items[m]) for m in range(len(items))]
        bit *= 2
    return items


def near_place(n_split, i):
    return [m for m in range(n_split) if m != 1].index(i)


def pack_kernel(n_split, occ_mask_hbm, virt_mask_hbm, b_hbm, occ_hbm, virt_hbm, virt_ref, *rest):
    outs, (occ_mask, virt_mask, b, occ_green, virt_green, sems) = rest[:n_split], rest[n_split:]
    pairs = (
        (b_hbm, b), (occ_hbm, occ_green), (virt_hbm, virt_green), (occ_mask_hbm, occ_mask), (virt_mask_hbm, virt_mask)
    )
    copies = [pltpu.make_async_copy(src, dst, sems.at[i]) for i, (src, dst) in enumerate(pairs)]
    for copy in copies:
        copy.start()
    s, t = lax.axis_index("split"), lax.axis_index("tensor")
    rows, cols, naux = b.shape
    group = cols // n_split
    block = occ_green.shape[1] // occ_mask.shape[0]
    for copy in copies[1:]:
        copy.wait()
    virt = screened(virt_green[...], virt_mask, t * (cols // block), block)
    virt_ref[...] = virt.astype(BF16)
    occ = screened(occ_green[...], occ_mask, s * (rows // block), block)
    occ = xor_blocks(occ, cols, t).astype(BF16)
    width = group * naux + occ.shape[1]
    for m in range(n_split):
        outs[m][:, group * naux:width] = occ
    copies[0].wait()
    basis = jnp.swapaxes(b[...], 0, 1)
    for l in range(group):
        tiles = swap_lane_blocks([basis[j * group + l] for j in range(n_split)], naux // n_split)
        tiles = xor_list(tiles, s)
        for m in range(n_split):
            outs[m][:, l * naux:(l + 1) * naux] = tiles[m]
            if m != 1:
                start = width + near_place(n_split, m) * group * naux + l * naux
                outs[1][:, start:start + naux] = tiles[m]


def add_kernel(*refs):
    refs[-1][...] = sum(r[...] for r in refs[:-1])


def others(n_split, m):
    return [i for i in range(n_split) if i // 2 != m // 2]


def write_rows(out, start, blocks):
    rows, at = out.shape[0], 0
    for block in blocks:
        height = block.shape[0]
        for c in range(0, block.shape[1], 128):
            column = start + at // rows * 128
            out[at % rows:at % rows + height, column:column + 128] = block[:, c:c + 128]
            at += height


def read_rows(ref, start, count, height, width):
    rows, at, blocks = ref.shape[0], 0, []
    for _ in range(count):
        tiles = []
        for c in range(0, width, 128):
            column = start + at // rows * 128
            tiles.append(ref[at % rows:at % rows + height, column:column + 128])
            at += height
        blocks.append(jnp.concatenate(tiles, axis=1))
    return blocks


def first_kernel(n_split, n_tensor, width, own_virt, *refs):
    own, got, rest = refs[:n_split], refs[n_split:2 * n_split - 1][::-1], refs[2 * n_split - 1:]
    shares = n_tensor // n_split
    fetched, firsts, raws = rest[:shares], rest[shares:shares + n_tensor], rest[shares + n_tensor:]
    whole = jnp.concatenate([p[:, :own[0].shape[1]] for p in (own[0], *got)], axis=0)
    first = lax.dot_general(
        whole[:, width:], whole[:, :width], (((0,), (0,)), ((), ())), preferred_element_type=F32
    )
    cols = first.shape[0] // n_tensor
    for k in range(n_tensor):
        firsts[k][...] = first[k * cols:(k + 1) * cols].astype(BF16)
    blocks = [f[...] for f in fetched]
    blocks[0] = jnp.where(lax.axis_index("split") == 0, own_virt[...], blocks[0])
    for p in range(1, n_split // 2):
        for n, i in enumerate(others(n_split, 2 * p)):
            raws[p - 1][:, n * width:(n + 1) * width] = own[i][:, :width]
        write_rows(raws[p - 1], (n_split - 2) * width, blocks)
    pieces = list(got[1:])
    for n, piece in enumerate(pieces):
        raws[-1][:, n * width:(n + 1) * width] = piece[:, :width]
    write_rows(raws[-1], len(pieces) * width, blocks)


def g_kernel(n_split, n_tensor, width, *refs):
    own, got, refs = refs[:n_split], refs[n_split:2 * n_split - 1], refs[2 * n_split - 1:]
    raws, core, own_core, out, virt = refs[:n_split - 2], *refs[n_split - 2:]
    cols, nao, naux = out.shape
    rows = core.shape[0]
    group = cols // n_split
    shares = n_tensor // n_split
    s = lax.axis_index("split")

    def piece(m, q):
        if m == 0:
            return own[q], 0
        if q == 0:
            return got[m - 1], 0
        if m == 1:
            return got[0], own[0].shape[1] + near_place(n_split, q ^ 1) * width
        if q == 1:
            return core, ((m ^ 1) - 2) * width
        return raws[m - 2], others(n_split, m).index(m ^ q) * width

    core_start = (n_split - 2) * width
    found = [read_rows(own_core, core_start, shares, cols, nao), read_rows(core, core_start, shares, cols, nao)]
    found += [read_rows(r, (n_split - 2) * width, shares, cols, nao) for r in raws]
    blocks = [tile for i in range(shares) for tile in xor_list([f[i] for f in found], s)]
    ordered = xor_blocks(jnp.concatenate(blocks, axis=0), rows, s)
    row = lax.broadcasted_iota(jnp.int32, (nao, nao), 0)
    column = lax.broadcasted_iota(jnp.int32, (nao, nao), 1)
    j, k, l = row // (n_tensor * group), row // group % n_tensor, row % group
    place = jnp.where(column == k * cols + j * group + l, 1.0, 0.0).astype(BF16)
    virt[...] = jnp.dot(place, ordered, preferred_element_type=F32).astype(BF16)
    part = min(nao, 256)

    @pl.loop(0, nao // part)
    def _(i):
        band = pl.ds(pl.multiple_of(i * part, part), part)
        left = virt[band, :]
        for l in range(group):
            right = []
            for q in range(n_split):
                tiles = []
                for m in range(n_split):
                    ref, n = piece(m, q)
                    tiles.append(ref[:, n + l * naux:n + (l + 1) * naux])
                right.append(jnp.concatenate(tiles, axis=0))
            made = jnp.dot(left, jnp.concatenate(right, axis=1), preferred_element_type=F32).astype(BF16)
            tiles = swap_lane_blocks([made[:, q * naux:(q + 1) * naux] for q in range(n_split)], naux // n_split)
            for j, tile in enumerate(tiles):
                out[j * group + l, band, :] = tile


def last_kernel(n_split, n_tensor, scale, g_ref, *refs):
    firsts, out = refs[:n_tensor][::-1], refs[n_tensor]
    naux = g_ref.shape[2]
    group = firsts[0].shape[1] // naux
    width = naux // n_split
    depth = n_tensor * group
    left = jnp.stack([f[:, l * naux:(l + 1) * naux] for f in firsts for l in range(group)])
    left = jnp.swapaxes(left, 0, 1).reshape(-1, naux)
    right = [g_ref[:, j * depth:(j + 1) * depth, :].reshape(-1, naux) for j in range(n_split)]
    total = lax.dot_general(
        left, jnp.concatenate(right, axis=1), (((0,), (0,)), ((), ())), preferred_element_type=F32
    )
    result = total[:width, :naux]
    for j in range(1, n_split):
        result = result + total[j * width:(j + 1) * width, j * naux:(j + 1) * naux]
    out[...] = xor_blocks(result * scale, width, lax.axis_index("split"))


def stages(count):
    bit, found = 1, []
    if (count.bit_length() - 1) % 2:
        bit, found = 2, [[1]]
    while bit < count:
        found.append([bit, 2 * bit, 3 * bit])
        bit *= 4
    return found


def local(three_centre, green_occ, green_virt, occ_mask, virt_mask, *, n_split, n_tensor):
    rows, cols, naux = three_centre.shape
    nao = green_occ.shape[1]
    packed_width = cols // n_split * naux
    count = n_split * n_tensor
    params = pltpu.CompilerParams(vmem_limit_bytes=VMEM_LIMIT)
    vmem = pl.BlockSpec(memory_space=pltpu.VMEM)
    hbm = pl.BlockSpec(memory_space=pltpu.HBM)

    def exchange(x, split_bits=0, tensor_bits=0):
        bits = split_bits * n_tensor + tensor_bits
        return lax.ppermute(x, ("split", "tensor"), [(d, d ^ bits) for d in range(count)])

    def fetch(x, j):
        pairs = [(s * n_tensor + t, s * n_tensor + (t ^ (j * n_split + s))) for s in range(n_split) for t in range(n_tensor)]
        return lax.ppermute(x, ("split", "tensor"), [(a, b) for a, b in pairs if a != b])

    arguments = [occ_mask, virt_mask, three_centre, green_occ, green_virt]
    virt, *packed = pl.pallas_call(
        functools.partial(pack_kernel, n_split),
        out_shape=[jax.ShapeDtypeStruct(green_virt.shape, BF16)]
        + [
            jax.ShapeDtypeStruct((rows, packed_width + nao + (m == 1) * (n_split - 1) * packed_width), BF16)
            for m in range(n_split)
        ],
        in_specs=[hbm] * 5,
        out_specs=[vmem] * (n_split + 1),
        scratch_shapes=[
            pltpu.SMEM(occ_mask.shape, jnp.int32),
            pltpu.SMEM(virt_mask.shape, jnp.int32),
            pltpu.VMEM(three_centre.shape, BF16),
            pltpu.VMEM(green_occ.shape, BF16),
            pltpu.VMEM(green_virt.shape, BF16),
            pltpu.SemaphoreType.DMA((5,)),
        ],
        compiler_params=params,
    )(*[pltpu.with_memory_space_constraint(x, pltpu.HBM) for x in arguments])
    received = [exchange(packed[m], split_bits=m) for m in range(1, n_split)]

    own = virt
    shares = n_tensor // n_split
    fetched = [fetch(virt, j) for j in range(shares)]

    virt_width = shares * nao * cols // rows
    widths = [(n_split - 2) * packed_width + virt_width] * (n_split // 2 - 1) + [(n_split - 2) * packed_width + virt_width]
    made = pl.pallas_call(
        functools.partial(first_kernel, n_split, n_tensor, packed_width),
        out_shape=[jax.ShapeDtypeStruct((cols, packed_width), BF16)] * n_tensor
        + [jax.ShapeDtypeStruct((rows, w), BF16) for w in widths],
        in_specs=[vmem] * (2 * n_split + shares),
        out_specs=[vmem] * (n_tensor + len(widths)),
        compiler_params=params,
    )(own, *packed, *received[::-1], *fetched)
    firsts, raws = made[:n_tensor], made[n_tensor:]

    moved = {}
    moved.update({m: exchange(raws[m // 2 - 1], split_bits=m) for m in range(2, n_split, 2)})
    got = {0: firsts[0]}
    ahead = [k for k in range(n_tensor - 1, 1, -1) if k != n_tensor // 2]
    got.update({k: exchange(firsts[k], tensor_bits=k) for k in ahead})
    later = [k for k in range(n_tensor - 1, 0, -1) if k not in ahead]
    evens = list(range(2, n_split, 2))
    tied = list(lax.optimization_barrier((*[got[k] for k in ahead], *[moved[m] for m in evens], raws[-1], *[firsts[k] for k in later])))
    got.update(zip(ahead, tied))
    moved.update(zip(evens, tied[len(ahead):]))
    moved[1] = exchange(tied.pop(len(ahead) + len(evens)), split_bits=1)
    firsts = dict(enumerate(firsts))
    firsts.update(zip(later, tied[len(ahead) + len(evens):]))
    got.update({k: exchange(firsts[k], tensor_bits=k) for k in later})
    got = [got[k] for k in range(n_tensor)]
    moved.update({m + 1: exchange(moved[m], split_bits=1) for m in range(2, n_split, 2)})
    moved = [moved[m] for m in range(2, n_split)] + [moved[1]]

    g = pl.pallas_call(
        functools.partial(g_kernel, n_split, n_tensor, packed_width),
        out_shape=jax.ShapeDtypeStruct((cols, nao, naux), BF16),
        in_specs=[vmem] * (3 * n_split - 1),
        out_specs=vmem,
        scratch_shapes=[pltpu.VMEM((nao, nao), BF16)],
        compiler_params=params,
    )(*packed, *received, *moved, raws[-1])

    total = pl.pallas_call(
        functools.partial(last_kernel, n_split, n_tensor, 1.0 / nao),
        out_shape=jax.ShapeDtypeStruct((naux // n_split, naux), F32),
        in_specs=[vmem] * (1 + n_tensor),
        out_specs=vmem,
        compiler_params=params,
    )(g, *got[::-1])
    for near in stages(n_tensor):
        got = [exchange(total, tensor_bits=k) for k in near]
        if near != stages(n_tensor)[-1]:
            total = pl.pallas_call(
                add_kernel,
                out_shape=jax.ShapeDtypeStruct(total.shape, F32),
                in_specs=[vmem] * (1 + len(got)),
                out_specs=vmem,
                compiler_params=params,
            )(total, *got)
        else:
            total = sum(got, total)
    return total


def solution(mesh):
    sizes = dict(mesh.shape)
    return jax.shard_map(
        functools.partial(local, n_split=sizes["split"], n_tensor=sizes["tensor"]),
        mesh=mesh,
        in_specs=(P("split", "tensor", None), P("split", None), P("tensor", None), P(), P()),
        out_specs=P("split", None),
        check_vma=False,
    )
```

```python
import functools

import jax
import jax.numpy as jnp
from jax import lax
from jax.experimental import pallas as pl
from jax.experimental.pallas import tpu as pltpu
from jax.sharding import PartitionSpec as P

VMEM_LIMIT = 40 * 1024 * 1024
BF16 = jnp.bfloat16
F32 = jnp.float32


def xor_blocks(x, width, index):
    cols = x.shape[1]
    bit = 1
    while width * bit < cols:
        span = width * bit
        order = []
        for start in range(0, cols, 2 * span):
            order += [x[:, start + span:start + 2 * span], x[:, start:start + span]]
        x = jnp.where((index & bit) != 0, jnp.concatenate(order, axis=1), x)
        bit *= 2
    return x


def screened(green, mask_ref, first_row, block):
    rows, cols = green.shape
    column = lax.broadcasted_iota(jnp.int32, (1, cols), 1) // block
    parts = []
    for r in range(rows // block):
        keep = jnp.zeros((1, cols), jnp.int32)
        for c in range(cols // block):
            keep = jnp.where(column == c, mask_ref[first_row + r, c], keep)
        part = green[r * block:(r + 1) * block].astype(F32)
        parts.append(jnp.where(keep > 0, part, 0.0))
    return jnp.concatenate(parts, axis=0) if len(parts) > 1 else parts[0]


def swap_lane_blocks(tiles, width):
    tiles = list(tiles)
    count = len(tiles)
    lanes = tiles[0].shape[1]
    lane = lax.broadcasted_iota(jnp.int32, tiles[0].shape, 1)
    half = count // 2
    while half:
        span = half * width
        low = (lane // span) % 2 == 0
        for j in range(count):
            if j & half:
                continue
            a, b = tiles[j], tiles[j | half]
            tiles[j] = jnp.where(low, a, pltpu.roll(b, span, 1))
            tiles[j | half] = jnp.where(low, pltpu.roll(a, lanes - span, 1), b)
        half //= 2
    return tiles


def xor_list(items, index):
    bit = 1
    while bit < len(items):
        flag = (index & bit) != 0
        items = [jnp.where(flag, items[m ^ bit], items[m]) for m in range(len(items))]
        bit *= 2
    return items


def near_place(n_split, i):
    return [m for m in range(n_split) if m != 1].index(i)


def pack_kernel(n_split, occ_mask_hbm, virt_mask_hbm, b_hbm, occ_hbm, virt_hbm, virt_ref, *rest):
    outs, (occ_mask, virt_mask, b, occ_green, virt_green, sems) = rest[:n_split], rest[n_split:]
    pairs = (
        (b_hbm, b), (occ_hbm, occ_green), (virt_hbm, virt_green), (occ_mask_hbm, occ_mask), (virt_mask_hbm, virt_mask)
    )
    copies = [pltpu.make_async_copy(src, dst, sems.at[i]) for i, (src, dst) in enumerate(pairs)]
    for copy in copies:
        copy.start()
    s, t = lax.axis_index("split"), lax.axis_index("tensor")
    rows, cols, naux = b.shape
    group = cols // n_split
    block = occ_green.shape[1] // occ_mask.shape[0]
    for copy in copies[1:]:
        copy.wait()
    virt = screened(virt_green[...], virt_mask, t * (cols // block), block)
    virt_ref[...] = virt.astype(BF16)
    occ = screened(occ_green[...], occ_mask, s * (rows // block), block)
    occ = xor_blocks(occ, cols, t).astype(BF16)
    width = group * naux + occ.shape[1]
    for m in range(n_split):
        outs[m][:, group * naux:width] = occ
    copies[0].wait()
    basis = jnp.swapaxes(b[...], 0, 1)
    for l in range(group):
        tiles = swap_lane_blocks([basis[j * group + l] for j in range(n_split)], naux // n_split)
        tiles = xor_list(tiles, s)
        for m in range(n_split):
            outs[m][:, l * naux:(l + 1) * naux] = tiles[m]
            if m != 1:
                start = width + near_place(n_split, m) * group * naux + l * naux
                outs[1][:, start:start + naux] = tiles[m]


def add_kernel(*refs):
    refs[-1][...] = sum(r[...] for r in refs[:-1])


def others(n_split, m):
    return [i for i in range(n_split) if i // 2 != m // 2]


def write_rows(out, start, blocks):
    rows, at = out.shape[0], 0
    for block in blocks:
        height = block.shape[0]
        for c in range(0, block.shape[1], 128):
            column = start + at // rows * 128
            out[at % rows:at % rows + height, column:column + 128] = block[:, c:c + 128]
            at += height


def read_rows(ref, start, count, height, width):
    rows, at, blocks = ref.shape[0], 0, []
    for _ in range(count):
        tiles = []
        for c in range(0, width, 128):
            column = start + at // rows * 128
            tiles.append(ref[at % rows:at % rows + height, column:column + 128])
            at += height
        blocks.append(jnp.concatenate(tiles, axis=1))
    return blocks


def first_kernel(n_split, n_tensor, width, own_virt, *refs):
    own, got, rest = refs[:n_split], refs[n_split:2 * n_split - 1][::-1], refs[2 * n_split - 1:]
    shares = n_tensor // n_split
    fetched, firsts, raws = rest[:shares], rest[shares:shares + n_tensor], rest[shares + n_tensor:]
    whole = jnp.concatenate([p[:, :own[0].shape[1]] for p in (own[0], *got)], axis=0)
    first = lax.dot_general(
        whole[:, width:], whole[:, :width], (((0,), (0,)), ((), ())), preferred_element_type=F32
    )
    cols = first.shape[0] // n_tensor
    for k in range(n_tensor):
        firsts[k][...] = first[k * cols:(k + 1) * cols].astype(BF16)
    blocks = [f[...] for f in fetched]
    blocks[0] = jnp.where(lax.axis_index("split") == 0, own_virt[...], blocks[0])
    for p in range(1, n_split // 2):
        for n, i in enumerate(others(n_split, 2 * p)):
            raws[p - 1][:, n * width:(n + 1) * width] = own[i][:, :width]
        write_rows(raws[p - 1], (n_split - 2) * width, blocks)
    pieces = list(got[1:])
    for n, piece in enumerate(pieces):
        raws[-1][:, n * width:(n + 1) * width] = piece[:, :width]
    write_rows(raws[-1], len(pieces) * width, blocks)


def g_kernel(n_split, n_tensor, width, *refs):
    own, got, refs = refs[:n_split], refs[n_split:2 * n_split - 1], refs[2 * n_split - 1:]
    raws, core, own_core, out, virt = refs[:n_split - 2], *refs[n_split - 2:]
    cols, nao, naux = out.shape
    rows = core.shape[0]
    group = cols // n_split
    shares = n_tensor // n_split
    s = lax.axis_index("split")

    def piece(m, q):
        if m == 0:
            return own[q], 0
        if q == 0:
            return got[m - 1], 0
        if m == 1:
            return got[0], own[0].shape[1] + near_place(n_split, q ^ 1) * width
        if q == 1:
            return core, ((m ^ 1) - 2) * width
        return raws[m - 2], others(n_split, m).index(m ^ q) * width

    core_start = (n_split - 2) * width
    found = [read_rows(own_core, core_start, shares, cols, nao), read_rows(core, core_start, shares, cols, nao)]
    found += [read_rows(r, (n_split - 2) * width, shares, cols, nao) for r in raws]
    blocks = [tile for i in range(shares) for tile in xor_list([f[i] for f in found], s)]
    ordered = xor_blocks(jnp.concatenate(blocks, axis=0), rows, s)
    row = lax.broadcasted_iota(jnp.int32, (nao, nao), 0)
    column = lax.broadcasted_iota(jnp.int32, (nao, nao), 1)
    j, k, l = row // (n_tensor * group), row // group % n_tensor, row % group
    place = jnp.where(column == k * cols + j * group + l, 1.0, 0.0).astype(BF16)
    virt[...] = jnp.dot(place, ordered, preferred_element_type=F32).astype(BF16)
    part = min(nao, 256)

    @pl.loop(0, nao // part)
    def _(i):
        band = pl.ds(pl.multiple_of(i * part, part), part)
        left = virt[band, :]
        for l in range(group):
            right = []
            for q in range(n_split):
                tiles = []
                for m in range(n_split):
                    ref, n = piece(m, q)
                    tiles.append(ref[:, n + l * naux:n + (l + 1) * naux])
                right.append(jnp.concatenate(tiles, axis=0))
            made = jnp.dot(left, jnp.concatenate(right, axis=1), preferred_element_type=F32).astype(BF16)
            tiles = swap_lane_blocks([made[:, q * naux:(q + 1) * naux] for q in range(n_split)], naux // n_split)
            for j, tile in enumerate(tiles):
                out[j * group + l, band, :] = tile


def last_kernel(n_split, n_tensor, scale, g_ref, *refs):
    firsts, out = refs[:n_tensor][::-1], refs[n_tensor]
    naux = g_ref.shape[2]
    group = firsts[0].shape[1] // naux
    width = naux // n_split
    depth = n_tensor * group
    left = jnp.stack([f[:, l * naux:(l + 1) * naux] for f in firsts for l in range(group)])
    left = jnp.swapaxes(left, 0, 1).reshape(-1, naux)
    right = [g_ref[:, j * depth:(j + 1) * depth, :].reshape(-1, naux) for j in range(n_split)]
    total = lax.dot_general(
        left, jnp.concatenate(right, axis=1), (((0,), (0,)), ((), ())), preferred_element_type=F32
    )
    result = total[:width, :naux]
    for j in range(1, n_split):
        result = result + total[j * width:(j + 1) * width, j * naux:(j + 1) * naux]
    out[...] = xor_blocks(result * scale, width, lax.axis_index("split"))


def stages(count):
    bit, found = 1, []
    if (count.bit_length() - 1) % 2:
        bit, found = 2, [[1]]
    while bit < count:
        found.append([bit, 2 * bit, 3 * bit])
        bit *= 4
    return found


def local(three_centre, green_occ, green_virt, occ_mask, virt_mask, *, n_split, n_tensor):
    rows, cols, naux = three_centre.shape
    nao = green_occ.shape[1]
    packed_width = cols // n_split * naux
    count = n_split * n_tensor
    params = pltpu.CompilerParams(vmem_limit_bytes=VMEM_LIMIT)
    vmem = pl.BlockSpec(memory_space=pltpu.VMEM)
    hbm = pl.BlockSpec(memory_space=pltpu.HBM)

    def exchange(x, split_bits=0, tensor_bits=0):
        bits = split_bits * n_tensor + tensor_bits
        return lax.ppermute(x, ("split", "tensor"), [(d, d ^ bits) for d in range(count)])

    def fetch(x, j):
        pairs = []
        for s in range(n_split):
            k = j * n_split + s
            pairs += [(s * n_tensor + t, s * n_tensor + (t ^ max(k, 1))) for t in range(n_tensor)]
        return lax.ppermute(x, ("split", "tensor"), pairs)

    arguments = [occ_mask, virt_mask, three_centre, green_occ, green_virt]
    virt, *packed = pl.pallas_call(
        functools.partial(pack_kernel, n_split),
        out_shape=[jax.ShapeDtypeStruct(green_virt.shape, BF16)]
        + [
            jax.ShapeDtypeStruct((rows, packed_width + nao + (m == 1) * (n_split - 1) * packed_width), BF16)
            for m in range(n_split)
        ],
        in_specs=[hbm] * 5,
        out_specs=[vmem] * (n_split + 1),
        scratch_shapes=[
            pltpu.SMEM(occ_mask.shape, jnp.int32),
            pltpu.SMEM(virt_mask.shape, jnp.int32),
            pltpu.VMEM(three_centre.shape, BF16),
            pltpu.VMEM(green_occ.shape, BF16),
            pltpu.VMEM(green_virt.shape, BF16),
            pltpu.SemaphoreType.DMA((5,)),
        ],
        compiler_params=params,
    )(*[pltpu.with_memory_space_constraint(x, pltpu.HBM) for x in arguments])
    received = [exchange(packed[m], split_bits=m) for m in range(1, n_split)]

    own = virt
    shares = n_tensor // n_split
    fetched = [fetch(virt, j) for j in range(shares)]

    virt_width = shares * nao * cols // rows
    widths = [(n_split - 2) * packed_width + virt_width] * (n_split // 2 - 1) + [(n_split - 2) * packed_width + virt_width]
    made = pl.pallas_call(
        functools.partial(first_kernel, n_split, n_tensor, packed_width),
        out_shape=[jax.ShapeDtypeStruct((cols, packed_width), BF16)] * n_tensor
        + [jax.ShapeDtypeStruct((rows, w), BF16) for w in widths],
        in_specs=[vmem] * (2 * n_split + shares),
        out_specs=[vmem] * (n_tensor + len(widths)),
        compiler_params=params,
    )(own, *packed, *received[::-1], *fetched)
    firsts, raws = made[:n_tensor], made[n_tensor:]

    moved = {}
    moved.update({m: exchange(raws[m // 2 - 1], split_bits=m) for m in range(2, n_split, 2)})
    got = {0: firsts[0]}
    far = range(n_tensor - 1, n_tensor // 2, -1)
    ahead = [k for k in far if k % 2] + [k for k in far if k % 2 == 0] + list(range(n_tensor // 2 - 1, 2, -1))
    got.update({k: exchange(firsts[k], tensor_bits=k) for k in ahead})
    later = [k for k in range(n_tensor - 1, 0, -1) if k not in ahead]
    evens = list(range(2, n_split, 2))
    tied = list(lax.optimization_barrier((*[got[k] for k in ahead], *[moved[m] for m in evens], raws[-1], *[firsts[k] for k in later])))
    got.update(zip(ahead, tied))
    moved.update(zip(evens, tied[len(ahead):]))
    moved[1] = exchange(tied.pop(len(ahead) + len(evens)), split_bits=1)
    firsts = dict(enumerate(firsts))
    firsts.update(zip(later, tied[len(ahead) + len(evens):]))
    got.update({k: exchange(firsts[k], tensor_bits=k) for k in later})
    got = [got[k] for k in range(n_tensor)]
    moved.update({m + 1: exchange(moved[m], split_bits=1) for m in range(2, n_split, 2)})
    moved = [moved[m] for m in range(2, n_split)] + [moved[1]]

    g = pl.pallas_call(
        functools.partial(g_kernel, n_split, n_tensor, packed_width),
        out_shape=jax.ShapeDtypeStruct((cols, nao, naux), BF16),
        in_specs=[vmem] * (3 * n_split - 1),
        out_specs=vmem,
        scratch_shapes=[pltpu.VMEM((nao, nao), BF16)],
        compiler_params=params,
    )(*packed, *received, *moved, raws[-1])

    total = pl.pallas_call(
        functools.partial(last_kernel, n_split, n_tensor, 1.0 / nao),
        out_shape=jax.ShapeDtypeStruct((naux // n_split, naux), F32),
        in_specs=[vmem] * (1 + n_tensor),
        out_specs=vmem,
        compiler_params=params,
    )(g, *got[::-1])
    for near in stages(n_tensor):
        got = [exchange(total, tensor_bits=k) for k in near]
        if near != stages(n_tensor)[-1]:
            total = pl.pallas_call(
                add_kernel,
                out_shape=jax.ShapeDtypeStruct(total.shape, F32),
                in_specs=[vmem] * (1 + len(got)),
                out_specs=vmem,
                compiler_params=params,
            )(total, *got)
        else:
            total = sum(got, total)
    return total


def solution(mesh):
    sizes = dict(mesh.shape)
    return jax.shard_map(
        functools.partial(local, n_split=sizes["split"], n_tensor=sizes["tensor"]),
        mesh=mesh,
        in_specs=(P("split", "tensor", None), P("split", None), P("tensor", None), P(), P()),
        out_specs=P("split", None),
        check_vma=False,
    )
```

```python
import functools

import jax
import jax.numpy as jnp
from jax import lax
from jax.experimental import pallas as pl
from jax.experimental.pallas import tpu as pltpu
from jax.sharding import PartitionSpec as P

VMEM_LIMIT = 40 * 1024 * 1024
CHUNKS, HALVES = 2, 2
BF16 = jnp.bfloat16
F32 = jnp.float32


def xor_blocks(x, width, index):
    cols = x.shape[1]
    bit = 1
    while width * bit < cols:
        span = width * bit
        order = []
        for start in range(0, cols, 2 * span):
            order += [x[:, start + span:start + 2 * span], x[:, start:start + span]]
        x = jnp.where((index & bit) != 0, jnp.concatenate(order, axis=1), x)
        bit *= 2
    return x


def screened(green, mask_ref, first_row, block):
    rows, cols = green.shape
    column = lax.broadcasted_iota(jnp.int32, (1, cols), 1) // block
    parts = []
    for r in range(rows // block):
        keep = jnp.zeros((1, cols), jnp.int32)
        for c in range(cols // block):
            keep = jnp.where(column == c, mask_ref[first_row + r, c], keep)
        part = green[r * block:(r + 1) * block].astype(F32)
        parts.append(jnp.where(keep > 0, part, 0.0))
    return jnp.concatenate(parts, axis=0) if len(parts) > 1 else parts[0]


def swap_lane_blocks(tiles, width):
    tiles = list(tiles)
    count = len(tiles)
    lanes = tiles[0].shape[1]
    lane = lax.broadcasted_iota(jnp.int32, tiles[0].shape, 1)
    half = count // 2
    while half:
        span = half * width
        low = (lane // span) % 2 == 0
        for j in range(count):
            if j & half:
                continue
            a, b = tiles[j], tiles[j | half]
            tiles[j] = jnp.where(low, a, pltpu.roll(b, span, 1))
            tiles[j | half] = jnp.where(low, pltpu.roll(a, lanes - span, 1), b)
        half //= 2
    return tiles


def xor_list(items, index):
    bit = 1
    while bit < len(items):
        flag = (index & bit) != 0
        items = [jnp.where(flag, items[m ^ bit], items[m]) for m in range(len(items))]
        bit *= 2
    return items


def near_place(n_split, i):
    return [m for m in range(n_split) if m != 1].index(i)


def pack_kernel(n_split, occ_mask_hbm, virt_mask_hbm, b_hbm, occ_hbm, virt_hbm, virt_ref, *rest):
    outs, (occ_mask, virt_mask, b, occ_green, virt_green, sems) = rest[:n_split], rest[n_split:]
    step = b.shape[0] // CHUNKS
    bands = [slice(i * step, (i + 1) * step) for i in range(CHUNKS)]
    pairs = [(occ_hbm, occ_green), (virt_hbm, virt_green), (occ_mask_hbm, occ_mask), (virt_mask_hbm, virt_mask)]
    pairs += [(b_hbm.at[band], b.at[band]) for band in bands]
    copies = [pltpu.make_async_copy(src, dst, sems.at[i]) for i, (src, dst) in enumerate(pairs)]
    for copy in copies:
        copy.start()
    s, t = lax.axis_index("split"), lax.axis_index("tensor")
    rows, cols, naux = b.shape
    group = cols // n_split
    block = occ_green.shape[1] // occ_mask.shape[0]
    for copy in copies[:4]:
        copy.wait()
    virt = screened(virt_green[...], virt_mask, t * (cols // block), block)
    virt_ref[...] = virt.astype(BF16)
    occ = screened(occ_green[...], occ_mask, s * (rows // block), block)
    occ = xor_blocks(occ, cols, t).astype(BF16)
    width = group * naux + occ.shape[1]
    for m in range(n_split):
        outs[m][:, group * naux:width] = occ
    half = rows // HALVES
    for first in range(0, rows, half):
        for i, copy in enumerate(copies[4:]):
            if first <= i * step < first + half:
                copy.wait()
        band = slice(first, first + half)
        basis = jnp.swapaxes(b[band], 0, 1)
        for l in range(group):
            tiles = swap_lane_blocks([basis[j * group + l] for j in range(n_split)], naux // n_split)
            tiles = xor_list(tiles, s)
            for m in range(n_split):
                outs[m][band, l * naux:(l + 1) * naux] = tiles[m]
                if m != 1:
                    start = width + near_place(n_split, m) * group * naux + l * naux
                    outs[1][band, start:start + naux] = tiles[m]


def add_kernel(*refs):
    refs[-1][...] = sum(r[...] for r in refs[:-1])


def others(n_split, m):
    return [i for i in range(n_split) if i // 2 != m // 2]


def write_rows(out, start, blocks):
    rows, at = out.shape[0], 0
    for block in blocks:
        height = block.shape[0]
        for c in range(0, block.shape[1], 128):
            column = start + at // rows * 128
            out[at % rows:at % rows + height, column:column + 128] = block[:, c:c + 128]
            at += height


def read_rows(ref, start, count, height, width):
    rows, at, blocks = ref.shape[0], 0, []
    for _ in range(count):
        tiles = []
        for c in range(0, width, 128):
            column = start + at // rows * 128
            tiles.append(ref[at % rows:at % rows + height, column:column + 128])
            at += height
        blocks.append(jnp.concatenate(tiles, axis=1))
    return blocks


def first_kernel(n_split, n_tensor, width, own_virt, *refs):
    own, got, rest = refs[:n_split], refs[n_split:2 * n_split - 1][::-1], refs[2 * n_split - 1:]
    shares = n_tensor // n_split
    fetched, firsts, raws = rest[:shares], rest[shares:shares + n_tensor], rest[shares + n_tensor:]
    whole = jnp.concatenate([p[:, :own[0].shape[1]] for p in (own[0], *got)], axis=0)
    first = lax.dot_general(
        whole[:, width:], whole[:, :width], (((0,), (0,)), ((), ())), preferred_element_type=F32
    )
    cols = first.shape[0] // n_tensor
    for k in range(n_tensor):
        firsts[k][...] = first[k * cols:(k + 1) * cols].astype(BF16)
    blocks = [f[...] for f in fetched]
    blocks[0] = jnp.where(lax.axis_index("split") == 0, own_virt[...], blocks[0])
    for p in range(1, n_split // 2):
        for n, i in enumerate(others(n_split, 2 * p)):
            raws[p - 1][:, n * width:(n + 1) * width] = own[i][:, :width]
        write_rows(raws[p - 1], (n_split - 2) * width, blocks)
    pieces = list(got[1:])
    for n, piece in enumerate(pieces):
        raws[-1][:, n * width:(n + 1) * width] = piece[:, :width]
    write_rows(raws[-1], len(pieces) * width, blocks)


def g_kernel(n_split, n_tensor, width, *refs):
    own, got, refs = refs[:n_split], refs[n_split:2 * n_split - 1], refs[2 * n_split - 1:]
    raws, core, own_core, out, virt = refs[:n_split - 2], *refs[n_split - 2:]
    cols, nao, naux = out.shape
    rows = core.shape[0]
    group = cols // n_split
    shares = n_tensor // n_split
    s = lax.axis_index("split")

    def piece(m, q):
        if m == 0:
            return own[q], 0
        if q == 0:
            return got[m - 1], 0
        if m == 1:
            return got[0], own[0].shape[1] + near_place(n_split, q ^ 1) * width
        if q == 1:
            return core, ((m ^ 1) - 2) * width
        return raws[m - 2], others(n_split, m).index(m ^ q) * width

    core_start = (n_split - 2) * width
    found = [read_rows(own_core, core_start, shares, cols, nao), read_rows(core, core_start, shares, cols, nao)]
    found += [read_rows(r, (n_split - 2) * width, shares, cols, nao) for r in raws]
    blocks = [tile for i in range(shares) for tile in xor_list([f[i] for f in found], s)]
    ordered = xor_blocks(jnp.concatenate(blocks, axis=0), rows, s)
    row = lax.broadcasted_iota(jnp.int32, (nao, nao), 0)
    column = lax.broadcasted_iota(jnp.int32, (nao, nao), 1)
    j, k, l = row // (n_tensor * group), row // group % n_tensor, row % group
    place = jnp.where(column == k * cols + j * group + l, 1.0, 0.0).astype(BF16)
    virt[...] = jnp.dot(place, ordered, preferred_element_type=F32).astype(BF16)
    part = min(nao, 256)

    @pl.loop(0, nao // part)
    def _(i):
        band = pl.ds(pl.multiple_of(i * part, part), part)
        left = virt[band, :]
        for l in range(group):
            right = []
            for q in range(n_split):
                tiles = []
                for m in range(n_split):
                    ref, n = piece(m, q)
                    tiles.append(ref[:, n + l * naux:n + (l + 1) * naux])
                right.append(jnp.concatenate(tiles, axis=0))
            made = jnp.dot(left, jnp.concatenate(right, axis=1), preferred_element_type=F32).astype(BF16)
            tiles = swap_lane_blocks([made[:, q * naux:(q + 1) * naux] for q in range(n_split)], naux // n_split)
            for j, tile in enumerate(tiles):
                out[j * group + l, band, :] = tile


def last_kernel(n_split, n_tensor, scale, g_ref, *refs):
    firsts, out = refs[:n_tensor][::-1], refs[n_tensor]
    naux = g_ref.shape[2]
    group = firsts[0].shape[1] // naux
    width = naux // n_split
    depth = n_tensor * group
    left = jnp.stack([f[:, l * naux:(l + 1) * naux] for f in firsts for l in range(group)])
    left = jnp.swapaxes(left, 0, 1).reshape(-1, naux)
    right = [g_ref[:, j * depth:(j + 1) * depth, :].reshape(-1, naux) for j in range(n_split)]
    total = lax.dot_general(
        left, jnp.concatenate(right, axis=1), (((0,), (0,)), ((), ())), preferred_element_type=F32
    )
    result = total[:width, :naux]
    for j in range(1, n_split):
        result = result + total[j * width:(j + 1) * width, j * naux:(j + 1) * naux]
    out[...] = xor_blocks(result * scale, width, lax.axis_index("split"))


def stages(count):
    bit, found = 1, []
    if (count.bit_length() - 1) % 2:
        bit, found = 2, [[1]]
    while bit < count:
        found.append([bit, 2 * bit, 3 * bit])
        bit *= 4
    return found


def local(three_centre, green_occ, green_virt, occ_mask, virt_mask, *, n_split, n_tensor):
    rows, cols, naux = three_centre.shape
    nao = green_occ.shape[1]
    packed_width = cols // n_split * naux
    count = n_split * n_tensor
    params = pltpu.CompilerParams(vmem_limit_bytes=VMEM_LIMIT)
    vmem = pl.BlockSpec(memory_space=pltpu.VMEM)
    hbm = pl.BlockSpec(memory_space=pltpu.HBM)

    def exchange(x, split_bits=0, tensor_bits=0):
        bits = split_bits * n_tensor + tensor_bits
        return lax.ppermute(x, ("split", "tensor"), [(d, d ^ bits) for d in range(count)])

    def fetch(x, j):
        pairs = []
        for s in range(n_split):
            k = j * n_split + s
            pairs += [(s * n_tensor + t, s * n_tensor + (t ^ max(k, 1))) for t in range(n_tensor)]
        return lax.ppermute(x, ("split", "tensor"), pairs)

    arguments = [occ_mask, virt_mask, three_centre, green_occ, green_virt]
    virt, *packed = pl.pallas_call(
        functools.partial(pack_kernel, n_split),
        out_shape=[jax.ShapeDtypeStruct(green_virt.shape, BF16)]
        + [
            jax.ShapeDtypeStruct((rows, packed_width + nao + (m == 1) * (n_split - 1) * packed_width), BF16)
            for m in range(n_split)
        ],
        in_specs=[hbm] * 5,
        out_specs=[vmem] * (n_split + 1),
        scratch_shapes=[
            pltpu.SMEM(occ_mask.shape, jnp.int32),
            pltpu.SMEM(virt_mask.shape, jnp.int32),
            pltpu.VMEM(three_centre.shape, BF16),
            pltpu.VMEM(green_occ.shape, BF16),
            pltpu.VMEM(green_virt.shape, BF16),
            pltpu.SemaphoreType.DMA((4 + CHUNKS,)),
        ],
        compiler_params=params,
    )(*[pltpu.with_memory_space_constraint(x, pltpu.HBM) for x in arguments])
    received = [exchange(packed[m], split_bits=m) for m in range(1, n_split)]

    own = virt
    shares = n_tensor // n_split
    fetched = [fetch(virt, j) for j in range(shares)]

    virt_width = shares * nao * cols // rows
    widths = [(n_split - 2) * packed_width + virt_width] * (n_split // 2 - 1) + [(n_split - 2) * packed_width + virt_width]
    made = pl.pallas_call(
        functools.partial(first_kernel, n_split, n_tensor, packed_width),
        out_shape=[jax.ShapeDtypeStruct((cols, packed_width), BF16)] * n_tensor
        + [jax.ShapeDtypeStruct((rows, w), BF16) for w in widths],
        in_specs=[vmem] * (2 * n_split + shares),
        out_specs=[vmem] * (n_tensor + len(widths)),
        compiler_params=params,
    )(own, *packed, *received[::-1], *fetched)
    firsts, raws = made[:n_tensor], made[n_tensor:]

    moved = {}
    moved.update({m: exchange(raws[m // 2 - 1], split_bits=m) for m in range(2, n_split, 2)})
    got = {0: firsts[0]}
    far = range(n_tensor - 1, n_tensor // 2, -1)
    ahead = [k for k in far if k % 2] + [k for k in far if k % 2 == 0] + list(range(n_tensor // 2 - 1, 2, -1))
    got.update({k: exchange(firsts[k], tensor_bits=k) for k in ahead})
    later = [k for k in range(n_tensor - 1, 0, -1) if k not in ahead]
    evens = list(range(2, n_split, 2))
    tied = list(lax.optimization_barrier((*[got[k] for k in ahead], *[moved[m] for m in evens], raws[-1], *[firsts[k] for k in later])))
    got.update(zip(ahead, tied))
    moved.update(zip(evens, tied[len(ahead):]))
    moved[1] = exchange(tied.pop(len(ahead) + len(evens)), split_bits=1)
    firsts = dict(enumerate(firsts))
    firsts.update(zip(later, tied[len(ahead) + len(evens):]))
    got.update({k: exchange(firsts[k], tensor_bits=k) for k in later})
    got = [got[k] for k in range(n_tensor)]
    moved.update({m + 1: exchange(moved[m], split_bits=1) for m in range(2, n_split, 2)})
    moved = [moved[m] for m in range(2, n_split)] + [moved[1]]

    g = pl.pallas_call(
        functools.partial(g_kernel, n_split, n_tensor, packed_width),
        out_shape=jax.ShapeDtypeStruct((cols, nao, naux), BF16),
        in_specs=[vmem] * (3 * n_split - 1),
        out_specs=vmem,
        scratch_shapes=[pltpu.VMEM((nao, nao), BF16)],
        compiler_params=params,
    )(*packed, *received, *moved, raws[-1])

    total = pl.pallas_call(
        functools.partial(last_kernel, n_split, n_tensor, 1.0 / nao),
        out_shape=jax.ShapeDtypeStruct((naux // n_split, naux), F32),
        in_specs=[vmem] * (1 + n_tensor),
        out_specs=vmem,
        compiler_params=params,
    )(g, *got[::-1])
    for near in stages(n_tensor):
        got = [exchange(total, tensor_bits=k) for k in near]
        if near != stages(n_tensor)[-1]:
            total = pl.pallas_call(
                add_kernel,
                out_shape=jax.ShapeDtypeStruct(total.shape, F32),
                in_specs=[vmem] * (1 + len(got)),
                out_specs=vmem,
                compiler_params=params,
            )(total, *got)
        else:
            total = sum(got, total)
    return total


def solution(mesh):
    sizes = dict(mesh.shape)
    return jax.shard_map(
        functools.partial(local, n_split=sizes["split"], n_tensor=sizes["tensor"]),
        mesh=mesh,
        in_specs=(P("split", "tensor", None), P("split", None), P("tensor", None), P(), P()),
        out_specs=P("split", None),
        check_vma=False,
    )
```

```python
import functools

import jax
import jax.numpy as jnp
from jax import lax
from jax.experimental import pallas as pl
from jax.experimental.pallas import tpu as pltpu
from jax.sharding import PartitionSpec as P

VMEM_LIMIT = 40 * 1024 * 1024
CHUNKS, HALVES = 2, 2
BF16 = jnp.bfloat16
F32 = jnp.float32


def xor_blocks(x, width, index):
    cols = x.shape[1]
    bit = 1
    while width * bit < cols:
        span = width * bit
        order = []
        for start in range(0, cols, 2 * span):
            order += [x[:, start + span:start + 2 * span], x[:, start:start + span]]
        x = jnp.where((index & bit) != 0, jnp.concatenate(order, axis=1), x)
        bit *= 2
    return x


def screened(green, mask_ref, first_row, block):
    rows, cols = green.shape
    column = lax.broadcasted_iota(jnp.int32, (1, cols), 1) // block
    parts = []
    for r in range(rows // block):
        keep = jnp.zeros((1, cols), jnp.int32)
        for c in range(cols // block):
            keep = jnp.where(column == c, mask_ref[first_row + r, c], keep)
        part = green[r * block:(r + 1) * block].astype(F32)
        parts.append(jnp.where(keep > 0, part, 0.0))
    return jnp.concatenate(parts, axis=0) if len(parts) > 1 else parts[0]


def swap_lane_blocks(tiles, width):
    tiles = list(tiles)
    count = len(tiles)
    lanes = tiles[0].shape[1]
    lane = lax.broadcasted_iota(jnp.int32, tiles[0].shape, 1)
    half = count // 2
    while half:
        span = half * width
        low = (lane // span) % 2 == 0
        for j in range(count):
            if j & half:
                continue
            a, b = tiles[j], tiles[j | half]
            tiles[j] = jnp.where(low, a, pltpu.roll(b, span, 1))
            tiles[j | half] = jnp.where(low, pltpu.roll(a, lanes - span, 1), b)
        half //= 2
    return tiles


def xor_list(items, index):
    bit = 1
    while bit < len(items):
        flag = (index & bit) != 0
        items = [jnp.where(flag, items[m ^ bit], items[m]) for m in range(len(items))]
        bit *= 2
    return items


def near_place(n_split, i):
    return [m for m in range(n_split) if m != 1].index(i)


def pack_kernel(n_split, occ_mask_hbm, virt_mask_hbm, b_hbm, occ_hbm, virt_hbm, virt_ref, *rest):
    outs, (occ_mask, virt_mask, b, occ_green, virt_green, sems) = rest[:n_split], rest[n_split:]
    step = b.shape[0] // CHUNKS
    bands = [slice(i * step, (i + 1) * step) for i in range(CHUNKS)]
    pairs = [(occ_hbm, occ_green), (virt_hbm, virt_green), (occ_mask_hbm, occ_mask), (virt_mask_hbm, virt_mask)]
    pairs += [(b_hbm.at[band], b.at[band]) for band in bands]
    copies = [pltpu.make_async_copy(src, dst, sems.at[i]) for i, (src, dst) in enumerate(pairs)]
    for copy in copies:
        copy.start()
    s, t = lax.axis_index("split"), lax.axis_index("tensor")
    rows, cols, naux = b.shape
    group = cols // n_split
    block = occ_green.shape[1] // occ_mask.shape[0]
    for copy in copies[:4]:
        copy.wait()
    virt = screened(virt_green[...], virt_mask, t * (cols // block), block)
    virt_ref[...] = virt.astype(BF16)
    occ = screened(occ_green[...], occ_mask, s * (rows // block), block)
    occ = xor_blocks(occ, cols, t).astype(BF16)
    width = group * naux + occ.shape[1]
    for m in range(n_split):
        outs[m][:, group * naux:width] = occ
    half = rows // HALVES
    for first in range(0, rows, half):
        for i, copy in enumerate(copies[4:]):
            if first <= i * step < first + half:
                copy.wait()
        band = slice(first, first + half)
        basis = jnp.swapaxes(b[band], 0, 1)
        for l in range(group):
            tiles = swap_lane_blocks([basis[j * group + l] for j in range(n_split)], naux // n_split)
            tiles = xor_list(tiles, s)
            for m in range(n_split):
                outs[m][band, l * naux:(l + 1) * naux] = tiles[m]
                if m != 1:
                    start = width + near_place(n_split, m) * group * naux + l * naux
                    outs[1][band, start:start + naux] = tiles[m]


def add_kernel(*refs):
    refs[-1][...] = sum(r[...] for r in refs[:-1])


def others(n_split, m):
    return [i for i in range(n_split) if i // 2 != m // 2]


def write_rows(out, start, blocks):
    rows, at = out.shape[0], 0
    for block in blocks:
        height = block.shape[0]
        for c in range(0, block.shape[1], 128):
            column = start + at // rows * 128
            out[at % rows:at % rows + height, column:column + 128] = block[:, c:c + 128]
            at += height


def read_rows(ref, start, count, height, width):
    rows, at, blocks = ref.shape[0], 0, []
    for _ in range(count):
        tiles = []
        for c in range(0, width, 128):
            column = start + at // rows * 128
            tiles.append(ref[at % rows:at % rows + height, column:column + 128])
            at += height
        blocks.append(jnp.concatenate(tiles, axis=1))
    return blocks


def first_kernel(n_split, n_tensor, width, own_virt, *refs):
    own, got, rest = refs[:n_split], refs[n_split:2 * n_split - 1][::-1], refs[2 * n_split - 1:]
    shares = n_tensor // n_split
    fetched, firsts, raws = rest[:shares], rest[shares:shares + n_tensor], rest[shares + n_tensor:]
    whole = jnp.concatenate([p[:, :own[0].shape[1]] for p in (own[0], *got)], axis=0)
    first = lax.dot_general(
        whole[:, width:], whole[:, :width], (((0,), (0,)), ((), ())), preferred_element_type=F32
    )
    cols = first.shape[0] // n_tensor
    for k in range(n_tensor):
        firsts[k][...] = first[k * cols:(k + 1) * cols].astype(BF16)
    blocks = [f[...] for f in fetched]
    blocks[0] = jnp.where(lax.axis_index("split") == 0, own_virt[...], blocks[0])
    for p in range(1, n_split // 2):
        for n, i in enumerate(others(n_split, 2 * p)):
            raws[p - 1][:, n * width:(n + 1) * width] = own[i][:, :width]
        write_rows(raws[p - 1], (n_split - 2) * width, blocks)
    pieces = list(got[1:])
    for n, piece in enumerate(pieces):
        raws[-1][:, n * width:(n + 1) * width] = piece[:, :width]
    write_rows(raws[-1], len(pieces) * width, blocks)


def g_kernel(n_split, n_tensor, width, *refs):
    own, got, refs = refs[:n_split], refs[n_split:2 * n_split - 1], refs[2 * n_split - 1:]
    raws, core, own_core, out, virt = refs[:n_split - 2], *refs[n_split - 2:]
    cols, nao, naux = out.shape
    rows = core.shape[0]
    group = cols // n_split
    shares = n_tensor // n_split
    s = lax.axis_index("split")

    def piece(m, q):
        if m == 0:
            return own[q], 0
        if q == 0:
            return got[m - 1], 0
        if m == 1:
            return got[0], own[0].shape[1] + near_place(n_split, q ^ 1) * width
        if q == 1:
            return core, ((m ^ 1) - 2) * width
        return raws[m - 2], others(n_split, m).index(m ^ q) * width

    core_start = (n_split - 2) * width
    found = [read_rows(own_core, core_start, shares, cols, nao), read_rows(core, core_start, shares, cols, nao)]
    found += [read_rows(r, (n_split - 2) * width, shares, cols, nao) for r in raws]
    blocks = [tile for i in range(shares) for tile in xor_list([f[i] for f in found], s)]
    ordered = xor_blocks(jnp.concatenate(blocks, axis=0), rows, s)
    row = lax.broadcasted_iota(jnp.int32, (nao, nao), 0)
    column = lax.broadcasted_iota(jnp.int32, (nao, nao), 1)
    j, k, l = row // (n_tensor * group), row // group % n_tensor, row % group
    place = jnp.where(column == k * cols + j * group + l, 1.0, 0.0).astype(BF16)
    virt[...] = jnp.dot(place, ordered, preferred_element_type=F32).astype(BF16)
    part = min(nao, 256)

    @pl.loop(0, nao // part)
    def _(i):
        band = pl.ds(pl.multiple_of(i * part, part), part)
        left = virt[band, :]
        for l in range(group):
            right = []
            for q in range(n_split):
                tiles = []
                for m in range(n_split):
                    ref, n = piece(m, q)
                    tiles.append(ref[:, n + l * naux:n + (l + 1) * naux])
                right.append(jnp.concatenate(tiles, axis=0))
            made = jnp.dot(left, jnp.concatenate(right, axis=1), preferred_element_type=F32).astype(BF16)
            tiles = swap_lane_blocks([made[:, q * naux:(q + 1) * naux] for q in range(n_split)], naux // n_split)
            for j, tile in enumerate(tiles):
                out[j * group + l, band, :] = tile


def last_kernel(n_split, n_tensor, scale, g_ref, *refs):
    firsts, out = refs[:n_tensor][::-1], refs[n_tensor]
    naux = g_ref.shape[2]
    group = firsts[0].shape[1] // naux
    width = naux // n_split
    depth = n_tensor * group
    left = jnp.stack([f[:, l * naux:(l + 1) * naux] for f in firsts for l in range(group)])
    left = jnp.swapaxes(left, 0, 1).reshape(-1, naux)
    right = [g_ref[:, j * depth:(j + 1) * depth, :].reshape(-1, naux) for j in range(n_split)]
    total = lax.dot_general(
        left, jnp.concatenate(right, axis=1), (((0,), (0,)), ((), ())), preferred_element_type=F32
    )
    result = total[:width, :naux]
    for j in range(1, n_split):
        result = result + total[j * width:(j + 1) * width, j * naux:(j + 1) * naux]
    out[...] = xor_blocks(result * scale, width, lax.axis_index("split"))


def stages(count):
    bit, found = 1, []
    if (count.bit_length() - 1) % 2:
        bit, found = 2, [[1]]
    while bit < count:
        found.append([2 * bit, bit, 3 * bit])
        bit *= 4
    return found


def local(three_centre, green_occ, green_virt, occ_mask, virt_mask, *, n_split, n_tensor):
    rows, cols, naux = three_centre.shape
    nao = green_occ.shape[1]
    packed_width = cols // n_split * naux
    count = n_split * n_tensor
    params = pltpu.CompilerParams(vmem_limit_bytes=VMEM_LIMIT)
    vmem = pl.BlockSpec(memory_space=pltpu.VMEM)
    hbm = pl.BlockSpec(memory_space=pltpu.HBM)

    def exchange(x, split_bits=0, tensor_bits=0):
        bits = split_bits * n_tensor + tensor_bits
        return lax.ppermute(x, ("split", "tensor"), [(d, d ^ bits) for d in range(count)])

    def fetch(x, j):
        pairs = []
        for s in range(n_split):
            k = j * n_split + s
            pairs += [(s * n_tensor + t, s * n_tensor + (t ^ max(k, 1))) for t in range(n_tensor)]
        return lax.ppermute(x, ("split", "tensor"), pairs)

    arguments = [occ_mask, virt_mask, three_centre, green_occ, green_virt]
    virt, *packed = pl.pallas_call(
        functools.partial(pack_kernel, n_split),
        out_shape=[jax.ShapeDtypeStruct(green_virt.shape, BF16)]
        + [
            jax.ShapeDtypeStruct((rows, packed_width + nao + (m == 1) * (n_split - 1) * packed_width), BF16)
            for m in range(n_split)
        ],
        in_specs=[hbm] * 5,
        out_specs=[vmem] * (n_split + 1),
        scratch_shapes=[
            pltpu.SMEM(occ_mask.shape, jnp.int32),
            pltpu.SMEM(virt_mask.shape, jnp.int32),
            pltpu.VMEM(three_centre.shape, BF16),
            pltpu.VMEM(green_occ.shape, BF16),
            pltpu.VMEM(green_virt.shape, BF16),
            pltpu.SemaphoreType.DMA((4 + CHUNKS,)),
        ],
        compiler_params=params,
    )(*[pltpu.with_memory_space_constraint(x, pltpu.HBM) for x in arguments])
    received = [exchange(packed[m], split_bits=m) for m in range(1, n_split)]

    own = virt
    shares = n_tensor // n_split
    fetched = [fetch(virt, j) for j in range(shares)]

    virt_width = shares * nao * cols // rows
    widths = [(n_split - 2) * packed_width + virt_width] * (n_split // 2 - 1) + [(n_split - 2) * packed_width + virt_width]
    made = pl.pallas_call(
        functools.partial(first_kernel, n_split, n_tensor, packed_width),
        out_shape=[jax.ShapeDtypeStruct((cols, packed_width), BF16)] * n_tensor
        + [jax.ShapeDtypeStruct((rows, w), BF16) for w in widths],
        in_specs=[vmem] * (2 * n_split + shares),
        out_specs=[vmem] * (n_tensor + len(widths)),
        compiler_params=params,
    )(own, *packed, *received[::-1], *fetched)
    firsts, raws = made[:n_tensor], made[n_tensor:]

    moved = {}
    moved.update({m: exchange(raws[m // 2 - 1], split_bits=m) for m in range(2, n_split, 2)})
    got = {0: firsts[0]}
    far = range(n_tensor - 1, n_tensor // 2, -1)
    ahead = [k for k in far if k % 2] + [k for k in far if k % 2 == 0] + list(range(n_tensor // 2 - 1, 2, -1))
    got.update({k: exchange(firsts[k], tensor_bits=k) for k in ahead})
    later = [k for k in range(n_tensor - 1, 0, -1) if k not in ahead]
    evens = list(range(2, n_split, 2))
    tied = list(lax.optimization_barrier((*[got[k] for k in ahead], *[moved[m] for m in evens], raws[-1], *[firsts[k] for k in later])))
    got.update(zip(ahead, tied))
    moved.update(zip(evens, tied[len(ahead):]))
    moved[1] = exchange(tied.pop(len(ahead) + len(evens)), split_bits=1)
    firsts = dict(enumerate(firsts))
    firsts.update(zip(later, tied[len(ahead) + len(evens):]))
    got.update({k: exchange(firsts[k], tensor_bits=k) for k in later})
    got = [got[k] for k in range(n_tensor)]
    moved.update({m + 1: exchange(moved[m], split_bits=1) for m in range(2, n_split, 2)})
    moved = [moved[m] for m in range(2, n_split)] + [moved[1]]

    g = pl.pallas_call(
        functools.partial(g_kernel, n_split, n_tensor, packed_width),
        out_shape=jax.ShapeDtypeStruct((cols, nao, naux), BF16),
        in_specs=[vmem] * (3 * n_split - 1),
        out_specs=vmem,
        scratch_shapes=[pltpu.VMEM((nao, nao), BF16)],
        compiler_params=params,
    )(*packed, *received, *moved, raws[-1])

    total = pl.pallas_call(
        functools.partial(last_kernel, n_split, n_tensor, 1.0 / nao),
        out_shape=jax.ShapeDtypeStruct((naux // n_split, naux), F32),
        in_specs=[vmem] * (1 + n_tensor),
        out_specs=vmem,
        compiler_params=params,
    )(g, *got[::-1])
    for near in stages(n_tensor):
        got = [exchange(total, tensor_bits=k) for k in near]
        if near != stages(n_tensor)[-1]:
            total = pl.pallas_call(
                add_kernel,
                out_shape=jax.ShapeDtypeStruct(total.shape, F32),
                in_specs=[vmem] * (1 + len(got)),
                out_specs=vmem,
                compiler_params=params,
            )(total, *got)
        else:
            total = sum(got, total)
    return total


def solution(mesh):
    sizes = dict(mesh.shape)
    return jax.shard_map(
        functools.partial(local, n_split=sizes["split"], n_tensor=sizes["tensor"]),
        mesh=mesh,
        in_specs=(P("split", "tensor", None), P("split", None), P("tensor", None), P(), P()),
        out_specs=P("split", None),
        check_vma=False,
    )
```
